32 devices in a mesh: gen: 4 (over y, core), bus: 8 (over z, x).
Axes of the slice: x: 2, y: 2, z: 4, core: 2. Of those that a mesh axis runs over, the one named last changes fastest.
Arguments:
- bus_price: float32 [16, 12, 4096], P(None, None, 'bus'), may hold values from -4 to 4
- bus_demand: float32 [16, 12, 4096], P('gen', None, 'bus'), may hold values from 0 to 2
- multipliers: float32 [2, 16, 12, 6144], P(None, 'gen', None, 'bus'), may hold values from 0 to 1
- line_limits: float32 [6144], P('bus'), may hold values from 0.3 to 3
- ptdf_blocks: bfloat16 [48, 16, 128, 128], P('bus'), may hold values from -0.125 to 0.125
- ptdf_pattern: int32 [48, 16], P('bus'), may hold values from 0 to 31, as said below
- gen_bus: int32 [512], P(('gen', 'bus')), may hold values from 0 to 4095, as said below
- state_counts: int32 [512], P(('gen', 'bus')), may hold values from 64 to 512, as said below
- transitions: int32 [512, 3, 512], P(('gen', 'bus')), may hold values from 0 to 511, as said below
- state_level: float32 [512, 512], P(('gen', 'bus')), may hold values from 0 to 3
- state_cost: float32 [512, 512], P(('gen', 'bus')), may hold values from 0 to 2
Outputs:
- new_multipliers: float32 [2, 16, 12, 6144], P(None, 'gen', None, 'bus')
- new_price: float32 [16, 12, 4096], P(None, None, 'bus')
The draws below stay inside these ranges and needn't reach their ends.
Inputs may be any that keep to these rules, and one draw needn't show every extreme that they name: Generator i sits in bus block (i // 16) % 8: gen_bus[i] // 512 equals that number. `state_counts`: among the generators of each aligned group of 16, at most 6 have a count above 256, and some group has exactly 6. `transitions`: every successor of a state below its generator's count is below that count; a state at or above the count has itself as every successor. `ptdf_pattern`: the 16 bus blocks named in one row are different.
All inputs are finite; a program needn't handle non-finite values.
Results may differ from the reference program's by a relative error of at most 0.0031.
Values may be sent and summed in bfloat16 or wider, within the bound.
No kernel may reach another device: no remote copies, remote signals or barrier semaphores. Data moves between devices by JAX's collectives and lax.ppermute only.
A program may use at most 128 MiB of HBM per device.

```python
import math
import jax
import jax.numpy as jnp
from jax import lax

STATES = 512
SUCC = 3
HOURS = 12
GEN_DEV = 16
BIG_DEV = 6
BLK = 128
NNZB = 16
BUS_DEV = 512
SCN = 16
GENS = 512
BUSES = 4096
LINES = 6144


def count_table(key):
    device_total = GENS // GEN_DEV
    subkeys = jax.random.split(jax.random.fold_in(key, 11), 5)
    big_number = jax.random.randint(subkeys[0], (device_total,), 0, BIG_DEV + 1)
    busiest = jax.random.randint(subkeys[1], (), 0, device_total)
    device_ids = jnp.arange(device_total, dtype=jnp.int32)
    big_number = jnp.where(device_ids == busiest, BIG_DEV, big_number)
    scores = jax.random.randint(subkeys[2], (device_total, GEN_DEV), 0, 1 << 20) * GEN_DEV + jnp.arange(GEN_DEV, dtype=jnp.int32)[None, :]
    rank_table = jnp.argsort(jnp.argsort(scores, axis=1), axis=1)
    large_counts = jax.random.randint(subkeys[3], (device_total, GEN_DEV), STATES // 2 + 1, STATES + 1)
    small_counts = jax.random.randint(subkeys[4], (device_total, GEN_DEV), STATES // 8, STATES // 2 + 1)
    counts = jnp.where(rank_table < big_number[:, None], large_counts, small_counts)
    on_busiest = (device_ids == busiest)[:, None]
    counts = jnp.where(on_busiest & (rank_table == 0), STATES, counts)
    counts = jnp.where(on_busiest & (rank_table == GEN_DEV - 1), STATES // 8, counts)
    return counts.reshape(GENS).astype(jnp.int32)


def draw_state_counts(key, part):
    return count_table(key)


def draw_transitions(key, part):
    counts = count_table(key)
    chosen = jax.random.randint(jax.random.fold_in(key, 12), (GENS, SUCC, STATES), 0, counts[:, None, None])
    state_ids = jnp.broadcast_to(jnp.arange(STATES, dtype=jnp.int32)[None, None, :], (GENS, SUCC, STATES))
    return jnp.where(state_ids < counts[:, None, None], chosen, state_ids).astype(jnp.int32)


def draw_gen_bus(key, part):
    gen_ids = jnp.arange(GENS, dtype=jnp.int32)
    block_ids = gen_ids // GEN_DEV % (BUSES // BUS_DEV)
    offsets = jax.random.randint(jax.random.fold_in(key, 14), (GENS,), 0, BUS_DEV)
    offsets = jnp.where(gen_ids == GENS - 1, BUS_DEV - 1, offsets)
    offsets = jnp.where(gen_ids == 0, 0, offsets)
    return (block_ids * BUS_DEV + offsets).astype(jnp.int32)


def draw_ptdf_pattern(key, part):
    block_total = BUSES // BLK
    line_total = LINES // BLK
    subkeys = jax.random.split(jax.random.fold_in(key, 15), line_total)

    def pick_row(row_key):
        return jax.random.permutation(row_key, block_total)[:NNZB]
    return jax.vmap(pick_row)(subkeys).astype(jnp.int32)


def block_levels(own_key, dims, shards, least, largest):
    level, own = 1.0, jax.random.fold_in(own_key, 6)
    for axis_at, parts in shards:
        steps = jnp.exp(jax.random.uniform(jax.random.fold_in(own, axis_at), (parts,), jnp.float32, least / len(shards), largest / len(shards)))
        level = level * jnp.repeat(steps, dims[axis_at] // parts).reshape([-1 if axis == axis_at else 1 for axis in range(len(dims))])
    return level


def scatter_about(stream_key, shape, scale, bound, pieces=(), kind=jnp.bfloat16):
    level = block_levels(stream_key, shape, pieces, -0.22, 0.18) if pieces else 1.0
    drawn = jax.random.normal(stream_key, shape, jnp.float32) * scale * level
    return jnp.minimum(jnp.maximum(drawn, -bound), bound).astype(kind)


def setup_inputs(seed: int = 0) -> dict:
    seeds = jax.random.split(jax.random.key(seed), 12)
    return {
        "bus_price": scatter_about(seeds[0], (SCN, HOURS, BUSES), 1.0, 4.0, ((2, 8),), jnp.float32),
        "bus_demand": jnp.clip(2.0 * jax.random.uniform(seeds[1], (SCN, HOURS, BUSES), jnp.float32) ** block_levels(seeds[1], (SCN, HOURS, BUSES), ((0, 4), (2, 8)), -0.2, 0.2), 0.0, 2.0),
        "multipliers": jnp.clip(1.0 * jax.random.uniform(seeds[2], (2, SCN, HOURS, LINES), jnp.float32) ** block_levels(seeds[2], (2, SCN, HOURS, LINES), ((1, 4), (3, 8)), -0.2, 0.2), 0.0, 1.0),
        "line_limits": jnp.clip(jnp.exp(math.log(3.0) - 2.3025851 * jax.random.uniform(seeds[3], (LINES,), jnp.float32) ** block_levels(seeds[3], (LINES,), ((0, 8),), -0.2, 0.2)), 0.3, 3.0),
        "ptdf_blocks": scatter_about(seeds[4], (LINES // BLK, NNZB, BLK, BLK), (NNZB * BLK) ** -0.5, 0.125, ((0, 8),)),
        "ptdf_pattern": draw_ptdf_pattern(jax.random.fold_in(seeds[11], 71), 0),
        "gen_bus": draw_gen_bus(jax.random.fold_in(seeds[11], 71), 0),
        "state_counts": draw_state_counts(jax.random.fold_in(seeds[11], 71), 0),
        "transitions": draw_transitions(jax.random.fold_in(seeds[11], 71), 0),
        "state_level": jnp.clip(3.0 * jax.random.uniform(seeds[9], (GENS, STATES), jnp.float32) ** block_levels(seeds[9], (GENS, STATES), ((0, 32),), -0.2, 0.2), 0.0, 3.0),
        "state_cost": jnp.clip(2.0 * jax.random.uniform(seeds[10], (GENS, STATES), jnp.float32) ** block_levels(seeds[10], (GENS, STATES), ((0, 32),), -0.2, 0.2), 0.0, 2.0),
    }


STEP_SIZE = 1.0


def rounded(values):
    return lax.optimization_barrier(values.astype(jnp.bfloat16)).astype(jnp.float32)


def one_generator(level_row, cost_row, state_total, successor, gen_prices):
    state_ids = jnp.arange(STATES, dtype=jnp.int32)
    valid_row = (state_ids < state_total).astype(jnp.float32)
    weights = valid_row[None, None, :] * jnp.exp(gen_prices[:, :, None] * level_row[None, None, :] - cost_row[None, None, :])
    weights = jnp.transpose(weights, (1, 0, 2))
    targets = successor.reshape(-1)
    branches = successor.shape[0]

    def push(state_now):
        spread_out = jnp.tile(rounded(state_now), (1, branches))
        return jnp.zeros_like(state_now).at[:, targets].add(spread_out)

    def pull(values):
        return jnp.sum(rounded(values)[:, successor], axis=1)

    opening = weights[0] / jnp.sum(weights[0], axis=-1, keepdims=True)

    def forward(state_now, present_weight):
        raised = push(state_now) * present_weight
        scale_now = jnp.sum(raised, axis=-1, keepdims=True)
        state_next = raised / scale_now
        return state_next, (state_next, scale_now)

    unused_state, (states_later, scales) = lax.scan(forward, opening, weights[1:])
    states_all = jnp.concatenate([opening[None], states_later], axis=0)

    def backward(back_now, inputs):
        present_weight, scale_now = inputs
        back_prev = pull(present_weight * back_now / scale_now)
        return back_prev, back_prev

    ones_back = jnp.ones_like(opening)
    unused_back, backs_earlier = lax.scan(backward, ones_back, (weights[1:], scales), reverse=True)
    backs_all = jnp.concatenate([backs_earlier, ones_back[None]], axis=0)
    combined_probability = states_all * backs_all
    output = jnp.sum(combined_probability * level_row[None, None, :], axis=-1) / jnp.sum(combined_probability, axis=-1)
    return jnp.transpose(output, (1, 0))


def reference(bus_price, bus_demand, multipliers, line_limits, ptdf_blocks, ptdf_pattern, gen_bus, state_counts, transitions, state_level, state_cost):
    gen_prices = jnp.transpose(jnp.take(bus_price, gen_bus, axis=2), (2, 0, 1))
    group_count = GENS // GEN_DEV
    members_all = (state_level, state_cost, state_counts, transitions, gen_prices)
    shaped = tuple(member.reshape((group_count, GEN_DEV) + member.shape[1:]) for member in members_all)

    def run_group(members):
        return jax.vmap(one_generator)(*members)

    generation = lax.map(run_group, shaped).reshape(GENS, SCN, HOURS)
    injections = jnp.zeros((SCN, HOURS, BUSES), jnp.float32).at[:, :, gen_bus].add(jnp.transpose(generation, (1, 2, 0)))
    net_blocks = rounded(injections - bus_demand).reshape(SCN, HOURS, BUSES // BLK, BLK)
    line_blocks = LINES // BLK

    def flow_block(members):
        block_ptdf, block_ids = members
        chosen = net_blocks[:, :, block_ids]
        return jnp.einsum('shkb,kbc->shc', chosen, block_ptdf.astype(jnp.float32))

    flows_all = lax.map(flow_block, (ptdf_blocks, ptdf_pattern))
    flows = jnp.transpose(flows_all, (1, 2, 0, 3)).reshape(SCN, HOURS, LINES)
    upper_old = multipliers[0]
    lower_old = multipliers[1]
    upper_new = jnp.maximum(0.0, upper_old + STEP_SIZE * (flows - line_limits[None, None, :]))
    lower_new = jnp.maximum(0.0, lower_old + STEP_SIZE * (-flows - line_limits[None, None, :]))
    change = rounded((upper_new - upper_old) - (lower_new - lower_old))
    change_blocks = jnp.transpose(change.reshape(SCN, HOURS, line_blocks, BLK), (2, 0, 1, 3))

    def add_block(accumulated, members):
        block_ptdf, block_ids, block_change = members
        spread = jnp.einsum('shc,kbc->shkb', block_change, block_ptdf.astype(jnp.float32))
        return accumulated.at[:, :, block_ids].add(spread), None

    initial = jnp.zeros((SCN, HOURS, BUSES // BLK, BLK), jnp.float32)
    price_change, unused_out = lax.scan(add_block, initial, (ptdf_blocks, ptdf_pattern, change_blocks))
    new_price = bus_price - price_change.reshape(SCN, HOURS, BUSES)
    return jnp.stack([upper_new, lower_new]), new_price
```

```python
import functools

import jax
import jax.numpy as jnp
from jax import lax
from jax.experimental import pallas as pl
from jax.experimental.pallas import tpu as pltpu
from jax.sharding import PartitionSpec as P

STATES = 512
HALF = 256
BLK = 128
NNZB = 16
GROUP = 16
BIG_GROUP = 6
LANES = 128
SUBLANES = 8
EXACT = lax.Precision.HIGHEST


def plan_kernel(
    counts_smem,
    bus_smem,
    price_ref,
    trans_ref,
    level_ref,
    cost_ref,
    out_ref,
    order,
    level_slot,
    cost_slot,
    gen_price,
    big_table,
    small_table,
    big_state,
    small_state,
):
    scn, hours, bus_dev = price_ref.shape
    gens = level_ref.shape[0]
    big_total = BIG_GROUP * (gens // GROUP)
    parts = out_ref.shape[0]
    scn_dev = scn // parts
    per_row = LANES // gens

    def place(gen, taken):
        big = (counts_smem[gen] > HALF).astype(jnp.int32)
        slot = jnp.where(big == 1, taken, gens - 1 - (gen - taken))
        order[slot] = gen
        return taken + big

    lax.fori_loop(0, gens, place, jnp.int32(0))

    lane = lax.broadcasted_iota(jnp.int32, (1, LANES), 1)
    local_row = jnp.zeros((1, LANES), jnp.int32)
    bus_row = jnp.zeros((1, LANES), jnp.int32)
    for slot in range(gens):
        local = lax.rem(bus_smem[order[slot]], bus_dev)
        local_row = jnp.where(lane == slot, local, local_row)
        bus_row = jnp.where(lane == slot, local, bus_row)
    chooser = (
        lax.broadcasted_iota(jnp.int32, (bus_dev, LANES), 0) == local_row
    ).astype(jnp.float32)
    for n in range(scn):
        gen_price[n] = lax.dot_general(
            price_ref[n],
            chooser,
            (((1,), (0,)), ((), ())),
            precision=EXACT,
            preferred_element_type=jnp.float32,
        )

    state_ids = lax.broadcasted_iota(jnp.int32, (1, STATES), 1)
    spans = []
    for slot in range(gens):
        gen = order[slot]
        span = STATES if slot < big_total else HALF
        spans.append(span)
        level_slot[slot] = jnp.broadcast_to(level_ref[pl.ds(gen, 1), :], (SUBLANES, STATES))
        cost_row = jnp.where(state_ids < counts_smem[gen], cost_ref[pl.ds(gen, 1), :], 1e30)
        cost_slot[slot] = jnp.broadcast_to(cost_row, (SUBLANES, STATES))
        successors = trans_ref[gen]
        table = big_table.at[slot] if slot < big_total else small_table.at[slot - big_total]
        for first in range(0, span, HALF):
            shifted = (successors[:, :span] - first).astype(jnp.float32).astype(jnp.bfloat16)
            rows = lax.broadcasted_iota(jnp.int32, (HALF, span), 0).astype(jnp.float32).astype(jnp.bfloat16)
            one = jnp.ones((HALF, span), jnp.bfloat16)
            none = jnp.zeros((HALF, span), jnp.bfloat16)
            total = none
            for branch in range(successors.shape[0]):
                total = total + jnp.where(rows == shifted[branch : branch + 1, :], one, none)
            table[pl.ds(first, HALF), :] = total

    def repeat_rows(block, copies):
        return block if copies == 1 else jnp.concatenate([block] * copies, axis=0)

    outs = [jnp.zeros((scn, LANES), jnp.float32) for _ in range(-(-hours // per_row))]
    for hour in range(hours - 1, -1, -1):
        chains = hours - 1 - hour
        for slot in range(gens):
            span = spans[slot]
            if slot < big_total:
                state, table = big_state.at[slot], big_table.at[slot]
            else:
                state, table = small_state.at[slot - big_total], small_table.at[slot - big_total]
            level = repeat_rows(level_slot[slot][:, :span], scn // SUBLANES)
            cost = repeat_rows(cost_slot[slot][:, :span], scn // SUBLANES)
            price = gen_price[:, hour, slot : slot + 1]
            weight = jnp.exp(price * level - cost)
            base = weight if chains == 0 else weight * state[:scn, :]
            total = jnp.sum(base, axis=-1, keepdims=True)
            if hour > 0:
                share = 1.0 / total
                base = base * share
                weight = weight * share
                pieces = [base.astype(jnp.bfloat16)]
                for chain in range(chains):
                    pieces.append(
                        (weight * state[(chain + 1) * scn : (chain + 2) * scn, :]).astype(jnp.bfloat16)
                    )
                pieces.append((base * level).astype(jnp.bfloat16))
                moved = jnp.dot(
                    jnp.concatenate(pieces, axis=0), table[...], preferred_element_type=jnp.float32
                )
                state[: (chains + 2) * scn, :] = moved
            else:
                for at in range(hours):
                    if at == 0:
                        marked = base * level
                    else:
                        chain = hours - 1 - at
                        marked = weight * state[(chain + 1) * scn : (chain + 2) * scn, :]
                    mean = jnp.sum(marked, axis=-1, keepdims=True) / total
                    here = lane == (at % per_row) * gens + slot
                    outs[at // per_row] = jnp.where(here, mean, outs[at // per_row])
    for slot in range(gens):
        here = lane == (hours % per_row) * gens + slot
        bus = jnp.sum(jnp.where(lane == slot, bus_row, 0)).astype(jnp.float32)
        outs[-1] = jnp.where(here, bus, outs[-1])
    for part in range(parts):
        for row, block in enumerate(outs):
            out_ref[part, row] = block[part * scn_dev : (part + 1) * scn_dev, :]


def run_plan(state_counts, gen_bus, bus_price, transitions, state_level, state_cost, parts):
    scn, hours, _ = bus_price.shape
    gens = state_level.shape[0]
    big_total = BIG_GROUP * (gens // GROUP)
    rows = -(-hours // (LANES // gens))
    smem = pl.BlockSpec(memory_space=pltpu.SMEM)
    vmem = pl.BlockSpec(memory_space=pltpu.VMEM)
    return pl.pallas_call(
        plan_kernel,
        out_shape=jax.ShapeDtypeStruct((parts, rows, scn // parts, LANES), jnp.float32),
        in_specs=[smem, smem, vmem, vmem, vmem, vmem],
        out_specs=vmem,
        scratch_shapes=[
            pltpu.SMEM((gens,), jnp.int32),
            pltpu.VMEM((gens, SUBLANES, STATES), jnp.float32),
            pltpu.VMEM((gens, SUBLANES, STATES), jnp.float32),
            pltpu.VMEM((scn, hours, LANES), jnp.float32),
            pltpu.VMEM((big_total, STATES, STATES), jnp.bfloat16),
            pltpu.VMEM((gens - big_total, HALF, HALF), jnp.bfloat16),
            pltpu.VMEM((big_total, (hours + 1) * scn, STATES), jnp.float32),
            pltpu.VMEM((gens - big_total, (hours + 1) * scn, HALF), jnp.float32),
        ],
        compiler_params=pltpu.CompilerParams(vmem_limit_bytes=56 * 2**20),
        name="plan",
    )(state_counts, gen_bus, bus_price, transitions, state_level, state_cost)


def shards(
    bus_price,
    bus_demand,
    multipliers,
    line_limits,
    ptdf_blocks,
    ptdf_pattern,
    gen_bus,
    state_counts,
    transitions,
    state_level,
    state_cost,
):
    scn_dev, hours, bus_dev = bus_demand.shape
    gen_index = lax.axis_index("gen")
    parts = lax.axis_size("gen")
    gens = state_level.shape[0]
    per_row = LANES // gens
    block_total = lax.axis_size("bus") * bus_dev // BLK
    plan = run_plan(
        state_counts, gen_bus, bus_price, transitions, state_level, state_cost, parts
    )
    received = lax.all_to_all(plan, "gen", split_axis=0, concat_axis=0, tiled=True)
    rows = received.shape[1]
    spread = received.reshape(parts, rows, scn_dev, per_row, gens)
    places = spread[:, hours // per_row, 0, hours % per_row, :].reshape(-1)
    hourly = jnp.transpose(spread, (2, 1, 3, 0, 4)).reshape(scn_dev, rows * per_row, parts * gens)[:, :hours]
    placing_rows = (places[:, None] == jnp.arange(bus_dev, dtype=jnp.float32)[None, :]).astype(jnp.float32)
    injections = jnp.einsum("rtg,gb->rtb", hourly, placing_rows, precision=EXACT)
    row_total = scn_dev * hours
    network_row_block = (injections - bus_demand).astype(jnp.bfloat16).reshape(row_total, bus_dev)
    line_blocks = ptdf_blocks.shape[0]
    wanted = ptdf_pattern.reshape(-1)
    piece_cols = lax.all_gather(network_row_block, "bus", axis=1, tiled=True)
    block_count = piece_cols.shape[1] // BLK
    block_ids = jnp.arange(block_count, dtype=jnp.int32)
    chooser = (wanted[:, None] == block_ids[None, :]).astype(jnp.bfloat16)
    blocked = piece_cols.reshape(piece_cols.shape[0], block_count, BLK)
    picked_blocks = jnp.einsum("rjb,mj->rmb", blocked, chooser, preferred_element_type=jnp.float32)
    gathered = picked_blocks.astype(jnp.bfloat16).reshape(row_total, line_blocks, NNZB, BLK)
    flows = jnp.einsum("rlkb,lkbc->rlc", gathered, ptdf_blocks, preferred_element_type=jnp.float32)
    flow_lines = flows.reshape(scn_dev, hours, line_blocks * BLK)
    upper_old = multipliers[0]
    lower_old = multipliers[1]
    upper_new = jnp.maximum(0.0, upper_old + (flow_lines - line_limits[None, None, :]))
    lower_new = jnp.maximum(0.0, lower_old + (-flow_lines - line_limits[None, None, :]))
    change = (
        (upper_new - upper_old - (lower_new - lower_old))
        .astype(jnp.bfloat16)
        .reshape(row_total, line_blocks, BLK)
    )
    spread = jnp.einsum("rlc,lkbc->rlkb", change, ptdf_blocks, preferred_element_type=jnp.float32)
    placing = (
        ptdf_pattern[:, :, None] == jnp.arange(block_total, dtype=jnp.int32)[None, None, :]
    ).astype(jnp.float32)
    partial_change = jnp.einsum("rlkb,lkj->rjb", spread, placing, precision=EXACT).reshape(
        scn_dev, hours, block_total * BLK
    )
    own_change = lax.psum_scatter(partial_change, "bus", scatter_dimension=2, tiled=True)
    own_price = lax.dynamic_slice_in_dim(bus_price, gen_index * scn_dev, scn_dev, 0)
    new_share = own_price - own_change
    new_price = lax.all_gather(new_share, "gen", axis=0, tiled=True)
    return (jnp.stack([upper_new, lower_new]), new_price)


def solution(mesh):
    in_specs = (
        P(None, None, "bus"),
        P("gen", None, "bus"),
        P(None, "gen", None, "bus"),
        P("bus"),
        P("bus", None, None, None),
        P("bus", None),
        P(("gen", "bus")),
        P(("gen", "bus")),
        P(("gen", "bus"), None, None),
        P(("gen", "bus"), None),
        P(("gen", "bus"), None),
    )
    out_specs = (P(None, "gen", None, "bus"), P(None, None, "bus"))
    return jax.shard_map(shards, mesh=mesh, in_specs=in_specs, out_specs=out_specs, check_vma=False)
```

```python
import functools

import jax
import jax.numpy as jnp
from jax import lax
from jax.experimental import pallas as pl
from jax.experimental.pallas import tpu as pltpu
from jax.sharding import PartitionSpec as P

STATES = 512
HALF = 256
BLK = 128
NNZB = 16
GROUP = 16
BIG_GROUP = 6
LANES = 128
SUBLANES = 8
EXACT = lax.Precision.HIGHEST


def plan_kernel(
    counts_smem,
    bus_smem,
    price_ref,
    trans_ref,
    level_ref,
    cost_ref,
    out_ref,
    order,
    level_slot,
    cost_slot,
    gen_price,
    big_table,
    small_table,
    big_state,
    small_state,
):
    scn, hours, bus_dev = price_ref.shape
    gens = level_ref.shape[0]
    big_total = BIG_GROUP * (gens // GROUP)
    parts = out_ref.shape[0]
    scn_dev = scn // parts
    per_row = LANES // gens

    def place(gen, taken):
        big = (counts_smem[gen] > HALF).astype(jnp.int32)
        slot = jnp.where(big == 1, taken, gens - 1 - (gen - taken))
        order[slot] = gen
        return taken + big

    lax.fori_loop(0, gens, place, jnp.int32(0))

    lane = lax.broadcasted_iota(jnp.int32, (1, LANES), 1)
    local_row = jnp.zeros((1, LANES), jnp.int32)
    bus_row = jnp.zeros((1, LANES), jnp.int32)
    for slot in range(gens):
        local = lax.rem(bus_smem[order[slot]], bus_dev)
        local_row = jnp.where(lane == slot, local, local_row)
        bus_row = jnp.where(lane == slot, local, bus_row)
    chooser = (
        lax.broadcasted_iota(jnp.int32, (bus_dev, LANES), 0) == local_row
    ).astype(jnp.float32)
    for n in range(scn):
        gen_price[n] = lax.dot_general(
            price_ref[n],
            chooser,
            (((1,), (0,)), ((), ())),
            precision=EXACT,
            preferred_element_type=jnp.float32,
        )

    state_ids = lax.broadcasted_iota(jnp.int32, (1, STATES), 1)
    spans = []
    for slot in range(gens):
        gen = order[slot]
        span = STATES if slot < big_total else HALF
        spans.append(span)
        level_slot[slot] = jnp.broadcast_to(level_ref[pl.ds(gen, 1), :], (SUBLANES, STATES))
        cost_row = jnp.where(state_ids < counts_smem[gen], cost_ref[pl.ds(gen, 1), :], 1e30)
        cost_slot[slot] = jnp.broadcast_to(cost_row, (SUBLANES, STATES))
        successors = trans_ref[gen]
        table = big_table.at[slot] if slot < big_total else small_table.at[slot - big_total]
        for first in range(0, span, HALF):
            shifted = (successors[:, :span] - first).astype(jnp.float32).astype(jnp.bfloat16)
            rows = lax.broadcasted_iota(jnp.int32, (HALF, span), 0).astype(jnp.float32).astype(jnp.bfloat16)
            one = jnp.ones((HALF, span), jnp.bfloat16)
            none = jnp.zeros((HALF, span), jnp.bfloat16)
            total = none
            for branch in range(successors.shape[0]):
                total = total + jnp.where(rows == shifted[branch : branch + 1, :], one, none)
            table[pl.ds(first, HALF), :] = total

    def repeat_rows(block, copies):
        return block if copies == 1 else jnp.concatenate([block] * copies, axis=0)

    outs = [jnp.zeros((scn, LANES), jnp.float32) for _ in range(-(-hours // per_row))]
    for hour in range(hours - 1, -1, -1):
        chains = hours - 1 - hour
        for slot in range(gens):
            span = spans[slot]
            if slot < big_total:
                state, table = big_state.at[slot], big_table.at[slot]
            else:
                state, table = small_state.at[slot - big_total], small_table.at[slot - big_total]
            level = repeat_rows(level_slot[slot][:, :span], scn // SUBLANES)
            cost = repeat_rows(cost_slot[slot][:, :span], scn // SUBLANES)
            price = gen_price[:, hour, slot : slot + 1]
            weight = jnp.exp(price * level - cost)
            base = weight if chains == 0 else weight * state[:scn, :]
            total = jnp.sum(base, axis=-1, keepdims=True)
            if hour > 0:
                share = 1.0 / total
                base = base * share
                weight = weight * share
                pieces = [base.astype(jnp.bfloat16)]
                for chain in range(chains):
                    pieces.append(
                        (weight * state[(chain + 1) * scn : (chain + 2) * scn, :]).astype(jnp.bfloat16)
                    )
                pieces.append((base * level).astype(jnp.bfloat16))
                moved = jnp.dot(
                    jnp.concatenate(pieces, axis=0), table[...], preferred_element_type=jnp.float32
                )
                state[: (chains + 2) * scn, :] = moved
            else:
                for at in range(hours):
                    if at == 0:
                        marked = base * level
                    else:
                        chain = hours - 1 - at
                        marked = weight * state[(chain + 1) * scn : (chain + 2) * scn, :]
                    mean = jnp.sum(marked, axis=-1, keepdims=True) / total
                    here = lane == (at % per_row) * gens + slot
                    outs[at // per_row] = jnp.where(here, mean, outs[at // per_row])
    for slot in range(gens):
        here = lane == (hours % per_row) * gens + slot
        bus = jnp.sum(jnp.where(lane == slot, bus_row, 0)).astype(jnp.float32)
        outs[-1] = jnp.where(here, bus, outs[-1])
    for part in range(parts):
        for row, block in enumerate(outs):
            out_ref[part, row] = block[part * scn_dev : (part + 1) * scn_dev, :]


def run_plan(state_counts, gen_bus, bus_price, transitions, state_level, state_cost, parts):
    scn, hours, _ = bus_price.shape
    gens = state_level.shape[0]
    big_total = BIG_GROUP * (gens // GROUP)
    rows = -(-hours // (LANES // gens))
    smem = pl.BlockSpec(memory_space=pltpu.SMEM)
    vmem = pl.BlockSpec(memory_space=pltpu.VMEM)
    return pl.pallas_call(
        plan_kernel,
        out_shape=jax.ShapeDtypeStruct((parts, rows, scn // parts, LANES), jnp.float32),
        in_specs=[smem, smem, vmem, vmem, vmem, vmem],
        out_specs=vmem,
        scratch_shapes=[
            pltpu.SMEM((gens,), jnp.int32),
            pltpu.VMEM((gens, SUBLANES, STATES), jnp.float32),
            pltpu.VMEM((gens, SUBLANES, STATES), jnp.float32),
            pltpu.VMEM((scn, hours, LANES), jnp.float32),
            pltpu.VMEM((big_total, STATES, STATES), jnp.bfloat16),
            pltpu.VMEM((gens - big_total, HALF, HALF), jnp.bfloat16),
            pltpu.VMEM((big_total, (hours + 1) * scn, STATES), jnp.float32),
            pltpu.VMEM((gens - big_total, (hours + 1) * scn, HALF), jnp.float32),
        ],
        compiler_params=pltpu.CompilerParams(vmem_limit_bytes=56 * 2**20),
        name="plan",
    )(state_counts, gen_bus, bus_price, transitions, state_level, state_cost)


def net_kernel(plan_ref, demand_ref, net_ref, *, gens):
    parts, rows, scn_dev, _ = plan_ref.shape
    _, hours, bus_dev = demand_ref.shape
    per_row = LANES // gens
    lane = lax.broadcasted_iota(jnp.int32, (1, LANES), 1)
    hour_of_lane = lax.broadcasted_iota(jnp.int32, (per_row, LANES), 1) // gens
    hour_of_row = lax.broadcasted_iota(jnp.int32, (per_row, LANES), 0)
    bus_ids = lax.broadcasted_iota(jnp.int32, (bus_dev, LANES), 0).astype(jnp.float32)
    bus_start = (hours % per_row) * gens
    left, places = [], []
    for part in range(parts):
        pieces = []
        for n in range(scn_dev):
            for row in range(rows):
                values = jnp.broadcast_to(plan_ref[part, row][n : n + 1, :], (per_row, LANES))
                keep = (hour_of_lane == hour_of_row) & (hour_of_row < hours - row * per_row)
                pieces.append(jnp.where(keep, values, 0.0))
        left.append(jnp.concatenate(pieces, axis=0))
        bus = plan_ref[part, rows - 1][:1, :]
        bus = jnp.where((lane >= bus_start) & (lane < bus_start + gens), bus, 0.0)
        bus = jnp.broadcast_to(bus, (SUBLANES, LANES))
        shift = gens
        while shift < LANES:
            bus = bus + pltpu.roll(bus, shift, 1)
            shift *= 2
        places.append((bus_ids == bus[:1, :]).astype(jnp.bfloat16))
    left = jnp.concatenate(left, axis=1)
    high = left.astype(jnp.bfloat16)
    rest = left - high.astype(jnp.float32)
    middle = rest.astype(jnp.bfloat16)
    low = (rest - middle.astype(jnp.float32)).astype(jnp.bfloat16)
    placed = lax.dot_general(
        jnp.concatenate([high, middle, low], axis=0),
        jnp.concatenate(places, axis=1),
        (((1,), (1,)), ((), ())),
        preferred_element_type=jnp.float32,
    )
    count = left.shape[0]
    injections = placed[:count] + (placed[count : 2 * count] + placed[2 * count :])
    stride = rows * per_row
    net = [injections[n * stride : n * stride + hours] - demand_ref[n] for n in range(scn_dev)]
    net_ref[...] = jnp.concatenate(net, axis=0).astype(jnp.bfloat16)


def line_kernel(
    pattern_smem,
    place_smem,
    own_ref,
    *refs,
    half,
):
    far_refs = refs[: half - 1]
    other_ref, blocks_ref, limits_ref, old_ref, new_ref, near_out, far_out, net_all, spread_all = refs[half - 1 :]
    line_blocks, branches = pattern_smem.shape
    _, scn_dev, hours, _ = old_ref.shape
    row_total, bus_dev = own_ref.shape
    per_dev = bus_dev // BLK
    me = place_smem[0]
    my_pair, my_side = me // 2, lax.rem(me, 2)

    net_all[0] = own_ref[...]
    for step in range(1, half):
        net_all[step] = far_refs[step - 1][...]
    for step in range(half):
        net_all[half + step] = other_ref[step]
    spread_all[...] = jnp.zeros(spread_all.shape, jnp.float32)

    def spot(line, branch):
        block = pattern_smem[line, branch]
        owner = block // per_dev
        column = pl.multiple_of(lax.rem(block, per_dev) * BLK, BLK)
        step = lax.rem(my_pair - owner // 2 + half, half)
        side = jnp.where(lax.rem(owner, 2) == my_side, 0, half)
        return side + step, column

    for line in range(line_blocks):
        spots = [spot(line, branch) for branch in range(branches)]
        picked = [net_all[at, :, pl.ds(column, BLK)] for at, column in spots]
        table = blocks_ref[line].reshape(branches * BLK, BLK)
        flow = jnp.dot(
            jnp.concatenate(picked, axis=1), table, preferred_element_type=jnp.float32
        )
        lanes = pl.ds(line * BLK, BLK)
        limit = limits_ref[:, lanes]
        changes = []
        for n in range(scn_dev):
            here = flow[n * hours : (n + 1) * hours]
            upper_old = old_ref[0, n, :, lanes]
            lower_old = old_ref[1, n, :, lanes]
            upper = jnp.maximum(0.0, upper_old + (here - limit))
            lower = jnp.maximum(0.0, lower_old + (-here - limit))
            new_ref[0, n, :, lanes] = upper
            new_ref[1, n, :, lanes] = lower
            changes.append((upper - upper_old) - (lower - lower_old))
        change = jnp.concatenate(changes, axis=0).astype(jnp.bfloat16)
        spread = lax.dot_general(
            change, table, (((1,), (1,)), ((), ())), preferred_element_type=jnp.float32
        )
        for branch, (at, column) in enumerate(spots):
            spread_all[at, :, pl.ds(column, BLK)] += spread[:, branch * BLK : (branch + 1) * BLK]
    near_out[...] = spread_all[:half]
    far_out[...] = spread_all[half:].astype(jnp.bfloat16)


def price_kernel(place_smem, price_ref, *refs):
    share_refs, out_ref = refs[:-1], refs[-1]
    scn, hours, _ = price_ref.shape
    parts = len(share_refs)
    scn_dev = scn // parts
    me = place_smem[0]
    for step, share in enumerate(share_refs):
        start = lax.rem(me - step + parts, parts) * scn_dev
        for n in range(scn_dev):
            change = share[n * hours : (n + 1) * hours, :].astype(jnp.float32)
            out_ref[start + n] = price_ref[start + n] - change


def shards(
    bus_price,
    bus_demand,
    multipliers,
    line_limits,
    ptdf_blocks,
    ptdf_pattern,
    gen_bus,
    state_counts,
    transitions,
    state_level,
    state_cost,
):
    scn_dev, hours, bus_dev = bus_demand.shape
    parts = lax.axis_size("gen")
    ring = lax.axis_size("bus")
    half = ring // 2
    gens = state_level.shape[0]
    row_total = scn_dev * hours
    gen_place = lax.axis_index("gen").astype(jnp.int32).reshape(1)
    bus_place = lax.axis_index("bus").astype(jnp.int32).reshape(1)
    smem = pl.BlockSpec(memory_space=pltpu.SMEM)
    vmem = pl.BlockSpec(memory_space=pltpu.VMEM)
    roomy = pltpu.CompilerParams(vmem_limit_bytes=56 * 2**20)
    pairs = [(i, i ^ 1) for i in range(ring)]

    def shifted(step):
        return [(i, (i + 2 * step) % ring) for i in range(ring)]

    plan = run_plan(state_counts, gen_bus, bus_price, transitions, state_level, state_cost, parts)
    received = lax.all_to_all(plan, "gen", split_axis=0, concat_axis=0, tiled=True)
    net = pl.pallas_call(
        functools.partial(net_kernel, gens=gens),
        out_shape=jax.ShapeDtypeStruct((row_total, bus_dev), jnp.bfloat16),
        in_specs=[vmem, vmem],
        out_specs=vmem,
        compiler_params=roomy,
        name="net",
    )(received, bus_demand)

    far = [lax.ppermute(net, "bus", shifted(step)) for step in range(1, half)]
    other = lax.ppermute(jnp.stack([net] + far), "bus", pairs)
    new_multipliers, near_part, far_part = pl.pallas_call(
        functools.partial(line_kernel, half=half),
        out_shape=(
            jax.ShapeDtypeStruct(multipliers.shape, jnp.float32),
            jax.ShapeDtypeStruct((half, row_total, bus_dev), jnp.float32),
            jax.ShapeDtypeStruct((half, row_total, bus_dev), jnp.bfloat16),
        ),
        in_specs=[smem, smem] + [vmem] * (half + 4),
        out_specs=(vmem, vmem, vmem),
        scratch_shapes=[
            pltpu.VMEM((ring, row_total, bus_dev), jnp.bfloat16),
            pltpu.VMEM((ring, row_total, bus_dev), jnp.float32),
        ],
        compiler_params=roomy,
        name="lines",
    )(ptdf_pattern, bus_place, net, *far, other, ptdf_blocks, line_limits.reshape(1, -1), multipliers)

    traded = lax.ppermute(far_part, "bus", pairs)
    own_change = near_part[0] + traded[0].astype(jnp.float32)
    for step in range(1, half):
        share = (near_part[step] + traded[step].astype(jnp.float32)).astype(jnp.bfloat16)
        own_change = own_change + lax.ppermute(share, "bus", shifted(half - step)).astype(jnp.float32)
    shares = [own_change] + [
        lax.ppermute(own_change, "gen", [(i, (i + step) % parts) for i in range(parts)])
        for step in range(1, parts)
    ]
    new_price = pl.pallas_call(
        price_kernel,
        out_shape=jax.ShapeDtypeStruct(bus_price.shape, jnp.float32),
        in_specs=[smem] + [vmem] * (parts + 1),
        out_specs=vmem,
        compiler_params=roomy,
        name="price",
    )(gen_place, bus_price, *shares)
    return (new_multipliers, new_price)


def solution(mesh):
    in_specs = (
        P(None, None, "bus"),
        P("gen", None, "bus"),
        P(None, "gen", None, "bus"),
        P("bus"),
        P("bus", None, None, None),
        P("bus", None),
        P(("gen", "bus")),
        P(("gen", "bus")),
        P(("gen", "bus"), None, None),
        P(("gen", "bus"), None),
        P(("gen", "bus"), None),
    )
    out_specs = (P(None, "gen", None, "bus"), P(None, None, "bus"))
    return jax.shard_map(shards, mesh=mesh, in_specs=in_specs, out_specs=out_specs, check_vma=False)
```

```python
import functools

import jax
import jax.numpy as jnp
from jax import lax
from jax.experimental import pallas as pl
from jax.experimental.pallas import tpu as pltpu
from jax.sharding import PartitionSpec as P

STATES = 512
HALF = 256
BLK = 128
NNZB = 16
GROUP = 16
BIG_GROUP = 6
LANES = 128
SUBLANES = 8
EXACT = lax.Precision.HIGHEST


def plan_kernel(
    counts_smem,
    bus_smem,
    price_ref,
    trans_ref,
    level_ref,
    cost_ref,
    out_ref,
    order,
    level_slot,
    cost_slot,
    gen_price,
    big_table,
    small_table,
    big_state,
    small_state,
):
    hours, scn, bus_dev = price_ref.shape
    gens = level_ref.shape[0]
    big_total = BIG_GROUP * (gens // GROUP)
    parts = out_ref.shape[0]
    scn_dev = scn // parts
    per_row = LANES // gens

    def place(gen, taken):
        big = (counts_smem[gen] > HALF).astype(jnp.int32)
        slot = jnp.where(big == 1, taken, gens - 1 - (gen - taken))
        order[slot] = gen
        return taken + big

    lax.fori_loop(0, gens, place, jnp.int32(0))

    lane = lax.broadcasted_iota(jnp.int32, (1, LANES), 1)
    local_row = jnp.zeros((1, LANES), jnp.int32)
    bus_row = jnp.zeros((1, LANES), jnp.int32)
    for slot in range(gens):
        local = lax.rem(bus_smem[order[slot]], bus_dev)
        local_row = jnp.where(lane == slot, local, local_row)
        bus_row = jnp.where(lane == slot, local, bus_row)
    chooser = (
        lax.broadcasted_iota(jnp.int32, (bus_dev, LANES), 0) == local_row
    ).astype(jnp.float32)
    for hour in range(hours):
        gen_price[hour] = lax.dot_general(
            price_ref[hour],
            chooser,
            (((1,), (0,)), ((), ())),
            precision=EXACT,
            preferred_element_type=jnp.float32,
        )

    state_ids = lax.broadcasted_iota(jnp.int32, (1, STATES), 1)
    spans = []
    for slot in range(gens):
        gen = order[slot]
        span = STATES if slot < big_total else HALF
        spans.append(span)
        level_slot[slot] = jnp.broadcast_to(level_ref[pl.ds(gen, 1), :], (SUBLANES, STATES))
        cost_row = jnp.where(state_ids < counts_smem[gen], cost_ref[pl.ds(gen, 1), :], 1e30)
        cost_slot[slot] = jnp.broadcast_to(cost_row, (SUBLANES, STATES))
        successors = [trans_ref[branch, pl.ds(gen, 1), :] for branch in range(trans_ref.shape[0])]
        table = big_table.at[slot] if slot < big_total else small_table.at[slot - big_total]
        for first in range(0, span, HALF):
            rows = lax.broadcasted_iota(jnp.int32, (HALF, span), 0).astype(jnp.float32).astype(jnp.bfloat16)
            one = jnp.ones((HALF, span), jnp.bfloat16)
            none = jnp.zeros((HALF, span), jnp.bfloat16)
            total = none
            for row in successors:
                shifted = (row[:, :span] - first).astype(jnp.float32).astype(jnp.bfloat16)
                total = total + jnp.where(rows == shifted, one, none)
            table[pl.ds(first, HALF), :] = total

    def repeat_rows(block, copies):
        return block if copies == 1 else jnp.concatenate([block] * copies, axis=0)

    outs = [jnp.zeros((scn, LANES), jnp.float32) for _ in range(-(-hours // per_row))]
    for hour in range(hours - 1, -1, -1):
        chains = hours - 1 - hour
        for slot in range(gens):
            span = spans[slot]
            if slot < big_total:
                state, table = big_state.at[slot], big_table.at[slot]
            else:
                state, table = small_state.at[slot - big_total], small_table.at[slot - big_total]
            level = repeat_rows(level_slot[slot][:, :span], scn // SUBLANES)
            cost = repeat_rows(cost_slot[slot][:, :span], scn // SUBLANES)
            price = gen_price[hour][:, slot : slot + 1]
            weight = jnp.exp(price * level - cost)
            base = weight if chains == 0 else weight * state[:scn, :]
            total = jnp.sum(base, axis=-1, keepdims=True)
            if hour > 0:
                share = 1.0 / total
                base = base * share
                weight = weight * share
                pieces = [base.astype(jnp.bfloat16)]
                for chain in range(chains):
                    pieces.append(
                        (weight * state[(chain + 1) * scn : (chain + 2) * scn, :]).astype(jnp.bfloat16)
                    )
                pieces.append((base * level).astype(jnp.bfloat16))
                moved = jnp.dot(
                    jnp.concatenate(pieces, axis=0), table[...], preferred_element_type=jnp.float32
                )
                state[: (chains + 2) * scn, :] = moved
            else:
                for at in range(hours):
                    if at == 0:
                        marked = base * level
                    else:
                        chain = hours - 1 - at
                        marked = weight * state[(chain + 1) * scn : (chain + 2) * scn, :]
                    mean = jnp.sum(marked, axis=-1, keepdims=True) / total
                    here = lane == (at % per_row) * gens + slot
                    outs[at // per_row] = jnp.where(here, mean, outs[at // per_row])
    for slot in range(gens):
        here = lane == (hours % per_row) * gens + slot
        bus = jnp.sum(jnp.where(lane == slot, bus_row, 0)).astype(jnp.float32)
        outs[-1] = jnp.where(here, bus, outs[-1])
    for part in range(parts):
        for row, block in enumerate(outs):
            out_ref[part, row] = block[part * scn_dev : (part + 1) * scn_dev, :]


def run_plan(state_counts, gen_bus, bus_price, transitions, state_level, state_cost, parts):
    hours, scn, _ = bus_price.shape
    gens = state_level.shape[0]
    big_total = BIG_GROUP * (gens // GROUP)
    rows = -(-hours // (LANES // gens))
    smem = pl.BlockSpec(memory_space=pltpu.SMEM)
    vmem = pl.BlockSpec(memory_space=pltpu.VMEM)
    return pl.pallas_call(
        plan_kernel,
        out_shape=jax.ShapeDtypeStruct((parts, rows, scn // parts, LANES), jnp.float32),
        in_specs=[smem, smem, vmem, vmem, vmem, vmem],
        out_specs=vmem,
        scratch_shapes=[
            pltpu.SMEM((gens,), jnp.int32),
            pltpu.VMEM((gens, SUBLANES, STATES), jnp.float32),
            pltpu.VMEM((gens, SUBLANES, STATES), jnp.float32),
            pltpu.VMEM((hours, scn, LANES), jnp.float32),
            pltpu.VMEM((big_total, STATES, STATES), jnp.bfloat16),
            pltpu.VMEM((gens - big_total, HALF, HALF), jnp.bfloat16),
            pltpu.VMEM((big_total, (hours + 1) * scn, STATES), jnp.float32),
            pltpu.VMEM((gens - big_total, (hours + 1) * scn, HALF), jnp.float32),
        ],
        compiler_params=pltpu.CompilerParams(vmem_limit_bytes=28 * 2**20),
        name="plan",
    )(state_counts, gen_bus, bus_price, transitions, state_level, state_cost)


def net_kernel(plan_ref, demand_ref, net_ref, *, gens):
    parts, rows, scn_dev, _ = plan_ref.shape
    hours, _, bus_dev = demand_ref.shape
    per_row = LANES // gens
    lane = lax.broadcasted_iota(jnp.int32, (1, LANES), 1)
    bus_ids = lax.broadcasted_iota(jnp.int32, (bus_dev, LANES), 0).astype(jnp.float32)

    def of_hour(hour):
        start = (hour % per_row) * gens
        return (lane >= start) & (lane < start + gens)

    left, places = [], []
    for part in range(parts):
        values = [plan_ref[part, row] for row in range(rows)]
        left.append(
            jnp.concatenate(
                [jnp.where(of_hour(hour), values[hour // per_row], 0.0) for hour in range(hours)], axis=0
            )
        )
        bus = jnp.where(of_hour(hours), values[-1][:1, :], 0.0)
        bus = jnp.broadcast_to(bus, (SUBLANES, LANES))
        shift = gens
        while shift < LANES:
            bus = bus + pltpu.roll(bus, shift, 1)
            shift *= 2
        places.append((bus_ids == bus[:1, :]).astype(jnp.bfloat16))
    left = jnp.concatenate(left, axis=1)
    high = left.astype(jnp.bfloat16)
    rest = left - high.astype(jnp.float32)
    middle = rest.astype(jnp.bfloat16)
    low = (rest - middle.astype(jnp.float32)).astype(jnp.bfloat16)
    placed = lax.dot_general(
        jnp.concatenate([high, middle, low], axis=0),
        jnp.concatenate(places, axis=1),
        (((1,), (1,)), ((), ())),
        preferred_element_type=jnp.float32,
    )
    count = left.shape[0]
    injections = placed[:count] + (placed[count : 2 * count] + placed[2 * count :])
    demand = jnp.concatenate([demand_ref[hour] for hour in range(hours)], axis=0)
    net_ref[...] = (injections - demand).astype(jnp.bfloat16)


def line_kernel(
    pattern_smem,
    place_smem,
    own_ref,
    *refs,
    half,
):
    far_refs = refs[: half - 1]
    other_ref, blocks_ref, limits_ref, old_ref, new_ref, near_out, far_out, net_all, spread_all = refs[half - 1 :]
    line_blocks, branches = pattern_smem.shape
    _, hours, scn_dev, _ = old_ref.shape
    row_total, bus_dev = own_ref.shape
    per_dev = bus_dev // BLK
    me = place_smem[0]
    my_pair, my_side = me // 2, lax.rem(me, 2)

    net_all[0] = own_ref[...]
    for step in range(1, half):
        net_all[step] = far_refs[step - 1][...]
    for step in range(half):
        net_all[half + step] = other_ref[step]
    spread_all[...] = jnp.zeros(spread_all.shape, jnp.float32)

    def spot(line, branch):
        block = pattern_smem[line, branch]
        owner = block // per_dev
        column = pl.multiple_of(lax.rem(block, per_dev) * BLK, BLK)
        step = lax.rem(my_pair - owner // 2 + half, half)
        side = jnp.where(lax.rem(owner, 2) == my_side, 0, half)
        return side + step, column

    for line in range(line_blocks):
        spots = [spot(line, branch) for branch in range(branches)]
        picked = [net_all[at, :, pl.ds(column, BLK)] for at, column in spots]
        table = blocks_ref[line].reshape(branches * BLK, BLK)
        flow = jnp.dot(
            jnp.concatenate(picked, axis=1), table, preferred_element_type=jnp.float32
        )
        lanes = pl.ds(line * BLK, BLK)
        limit = limits_ref[lanes].reshape(1, BLK)
        upper_old = jnp.concatenate([old_ref[0, hour, :, lanes] for hour in range(hours)], axis=0)
        lower_old = jnp.concatenate([old_ref[1, hour, :, lanes] for hour in range(hours)], axis=0)
        upper = jnp.maximum(0.0, upper_old + (flow - limit))
        lower = jnp.maximum(0.0, lower_old + (-flow - limit))
        for hour in range(hours):
            here = slice(hour * scn_dev, (hour + 1) * scn_dev)
            new_ref[0, hour, :, lanes] = upper[here]
            new_ref[1, hour, :, lanes] = lower[here]
        change = ((upper - upper_old) - (lower - lower_old)).astype(jnp.bfloat16)
        spread = lax.dot_general(
            change, table, (((1,), (1,)), ((), ())), preferred_element_type=jnp.float32
        )
        for branch, (at, column) in enumerate(spots):
            spread_all[at, :, pl.ds(column, BLK)] += spread[:, branch * BLK : (branch + 1) * BLK]
    near_out[...] = spread_all[:half]
    far_out[...] = spread_all[half:].astype(jnp.bfloat16)


def price_kernel(place_smem, price_ref, *refs):
    share_refs, (out_ref, share_all) = refs[:-2], refs[-2:]
    hours, scn, _ = price_ref.shape
    parts = len(share_refs)
    scn_dev = scn // parts
    me = place_smem[0]
    for step, share in enumerate(share_refs):
        share_all[step] = share[...]
    steps = [lax.rem(me - part + parts, parts) for part in range(parts)]
    for hour in range(hours):
        change = [share_all[step, hour * scn_dev : (hour + 1) * scn_dev, :] for step in steps]
        out_ref[hour] = price_ref[hour] - jnp.concatenate(change, axis=0)


def shards(
    bus_price,
    bus_demand,
    multipliers,
    line_limits,
    ptdf_blocks,
    ptdf_pattern,
    gen_bus,
    state_counts,
    transitions,
    state_level,
    state_cost,
):
    scn_dev, hours, bus_dev = bus_demand.shape
    parts = lax.axis_size("gen")
    ring = lax.axis_size("bus")
    half = ring // 2
    gens = state_level.shape[0]
    row_total = scn_dev * hours
    gen_place = lax.axis_index("gen").astype(jnp.int32).reshape(1)
    bus_place = lax.axis_index("bus").astype(jnp.int32).reshape(1)
    smem = pl.BlockSpec(memory_space=pltpu.SMEM)
    vmem = pl.BlockSpec(memory_space=pltpu.VMEM)
    roomy = pltpu.CompilerParams(vmem_limit_bytes=24 * 2**20)
    pairs = [(i, i ^ 1) for i in range(ring)]

    def shifted(step):
        return [(i, (i + 2 * step) % ring) for i in range(ring)]

    bus_price = jnp.transpose(bus_price, (1, 0, 2))
    bus_demand = jnp.transpose(bus_demand, (1, 0, 2))
    multipliers = jnp.transpose(multipliers, (0, 2, 1, 3))
    transitions = jnp.transpose(transitions, (1, 0, 2))
    plan = run_plan(state_counts, gen_bus, bus_price, transitions, state_level, state_cost, parts)
    received = lax.all_to_all(plan, "gen", split_axis=0, concat_axis=0, tiled=True)
    net = pl.pallas_call(
        functools.partial(net_kernel, gens=gens),
        out_shape=jax.ShapeDtypeStruct((row_total, bus_dev), jnp.bfloat16),
        in_specs=[vmem, vmem],
        out_specs=vmem,
        compiler_params=roomy,
        name="net",
    )(received, bus_demand)

    far = [lax.ppermute(net, "bus", shifted(step)) for step in range(1, half)]
    other = lax.ppermute(jnp.stack([net] + far), "bus", pairs)
    new_multipliers, near_part, far_part = pl.pallas_call(
        functools.partial(line_kernel, half=half),
        out_shape=(
            jax.ShapeDtypeStruct(multipliers.shape, jnp.float32),
            jax.ShapeDtypeStruct((half, row_total, bus_dev), jnp.float32),
            jax.ShapeDtypeStruct((half, row_total, bus_dev), jnp.bfloat16),
        ),
        in_specs=[smem, smem] + [vmem] * (half + 4),
        out_specs=(vmem, vmem, vmem),
        scratch_shapes=[
            pltpu.VMEM((ring, row_total, bus_dev), jnp.bfloat16),
            pltpu.VMEM((ring, row_total, bus_dev), jnp.float32),
        ],
        compiler_params=roomy,
        name="lines",
    )(ptdf_pattern, bus_place, net, *far, other, ptdf_blocks, line_limits, multipliers)

    traded = lax.ppermute(far_part, "bus", pairs)
    own_change = near_part[0] + traded[0].astype(jnp.float32)
    for step in range(1, half):
        share = (near_part[step] + traded[step].astype(jnp.float32)).astype(jnp.bfloat16)
        own_change = own_change + lax.ppermute(share, "bus", shifted(half - step)).astype(jnp.float32)
    shares = [own_change] + [
        lax.ppermute(own_change, "gen", [(i, (i + step) % parts) for i in range(parts)])
        for step in range(1, parts)
    ]
    new_price = pl.pallas_call(
        price_kernel,
        out_shape=jax.ShapeDtypeStruct(bus_price.shape, jnp.float32),
        in_specs=[smem] + [vmem] * (parts + 1),
        out_specs=vmem,
        scratch_shapes=[pltpu.VMEM((parts, row_total, bus_dev), jnp.float32)],
        compiler_params=roomy,
        name="price",
    )(gen_place, bus_price, *shares)
    return (jnp.transpose(new_multipliers, (0, 2, 1, 3)), jnp.transpose(new_price, (1, 0, 2)))


def solution(mesh):
    in_specs = (
        P(None, None, "bus"),
        P("gen", None, "bus"),
        P(None, "gen", None, "bus"),
        P("bus"),
        P("bus", None, None, None),
        P("bus", None),
        P(("gen", "bus")),
        P(("gen", "bus")),
        P(("gen", "bus"), None, None),
        P(("gen", "bus"), None),
        P(("gen", "bus"), None),
    )
    out_specs = (P(None, "gen", None, "bus"), P(None, None, "bus"))
    return jax.shard_map(shards, mesh=mesh, in_specs=in_specs, out_specs=out_specs, check_vma=False)
```

```python
import functools

import jax
import jax.numpy as jnp
from jax import lax
from jax.experimental import pallas as pl
from jax.experimental.pallas import tpu as pltpu
from jax.sharding import PartitionSpec as P

STATES = 512
HALF = 256
BLK = 128
NNZB = 16
GROUP = 16
BIG_GROUP = 6
LANES = 128
AHEAD = 5
SUBLANES = 8
EXACT = lax.Precision.HIGHEST


def plan_kernel(*refs, gens, parts):
    (counts_hbm, bus_hbm, trans_hbm, level_hbm, cost_hbm, price_hbm), refs = refs[:6], refs[6:]
    ahead_hbm, refs = refs[:AHEAD], refs[AHEAD:]
    out_ref, refs = refs[0], refs[1:]
    ahead_refs, refs = refs[:AHEAD], refs[AHEAD:]
    (
        counts_smem,
        bus_smem,
        trans_ref,
        level_ref,
        cost_ref,
        price_ref,
        order,
        level_slot,
        cost_slot,
        gen_price,
        big_table,
        small_table,
        big_state,
        small_state,
        sems,
    ) = refs
    sources = (counts_hbm, bus_hbm, trans_hbm, level_hbm, cost_hbm, price_hbm) + ahead_hbm
    targets = (counts_smem, bus_smem, trans_ref, level_ref, cost_ref, price_ref) + ahead_refs
    copies = [
        pltpu.make_async_copy(source, target, sems.at[at])
        for at, (source, target) in enumerate(zip(sources, targets))
    ]
    for copy in copies:
        copy.start()
    hours, scn, bus_dev = price_ref.shape
    big_total = BIG_GROUP * (gens // GROUP)
    scn_dev = scn // parts
    per_row = LANES // gens
    for copy in copies[:2]:
        copy.wait()

    def place(gen, taken):
        big = (counts_smem[gen] > HALF).astype(jnp.int32)
        slot = jnp.where(big == 1, taken, gens - 1 - (gen - taken))
        order[slot] = gen
        return taken + big

    lax.fori_loop(0, gens, place, jnp.int32(0))

    for copy in copies[2:6]:
        copy.wait()
    lane = lax.broadcasted_iota(jnp.int32, (1, LANES), 1)
    local_row = jnp.zeros((1, LANES), jnp.int32)
    bus_row = jnp.zeros((1, LANES), jnp.int32)
    for slot in range(gens):
        local = lax.rem(bus_smem[order[slot]], bus_dev)
        local_row = jnp.where(lane == slot, local, local_row)
        bus_row = jnp.where(lane == slot, local, bus_row)
    chooser = (
        lax.broadcasted_iota(jnp.int32, (bus_dev, LANES), 0) == local_row
    ).astype(jnp.float32)
    for hour in range(hours):
        gen_price[hour] = lax.dot_general(
            price_ref[hour],
            chooser,
            (((1,), (0,)), ((), ())),
            precision=EXACT,
            preferred_element_type=jnp.float32,
        )

    state_ids = lax.broadcasted_iota(jnp.int32, (1, STATES), 1)
    spans = []
    for slot in range(gens):
        gen = order[slot]
        span = STATES if slot < big_total else HALF
        spans.append(span)
        level_slot[slot] = jnp.broadcast_to(level_ref[pl.ds(gen, 1), :], (SUBLANES, STATES))
        cost_row = jnp.where(state_ids < counts_smem[gen], cost_ref[pl.ds(gen, 1), :], 1e30)
        cost_slot[slot] = jnp.broadcast_to(cost_row, (SUBLANES, STATES))
        successors = [trans_ref[branch, pl.ds(gen, 1), :] for branch in range(trans_ref.shape[0])]
        table = big_table.at[slot] if slot < big_total else small_table.at[slot - big_total]
        for first in range(0, span, HALF):
            rows = lax.broadcasted_iota(jnp.int32, (HALF, span), 0).astype(jnp.float32).astype(jnp.bfloat16)
            one = jnp.ones((HALF, span), jnp.bfloat16)
            none = jnp.zeros((HALF, span), jnp.bfloat16)
            total = none
            for row in successors:
                shifted = (row[:, :span] - first).astype(jnp.float32).astype(jnp.bfloat16)
                total = total + jnp.where(rows == shifted, one, none)
            table[pl.ds(first, HALF), :] = total

    def repeat_rows(block, copies):
        return block if copies == 1 else jnp.concatenate([block] * copies, axis=0)

    outs = [jnp.zeros((scn, LANES), jnp.float32) for _ in range(-(-hours // per_row))]
    for hour in range(hours - 1, -1, -1):
        chains = hours - 1 - hour
        for slot in range(gens):
            span = spans[slot]
            if slot < big_total:
                state, table = big_state.at[slot], big_table.at[slot]
            else:
                state, table = small_state.at[slot - big_total], small_table.at[slot - big_total]
            level = repeat_rows(level_slot[slot][:, :span], scn // SUBLANES)
            cost = repeat_rows(cost_slot[slot][:, :span], scn // SUBLANES)
            price = gen_price[hour][:, slot : slot + 1]
            weight = jnp.exp(price * level - cost)
            base = weight if chains == 0 else weight * state[:scn, :]
            total = jnp.sum(base, axis=-1, keepdims=True)
            if hour > 0:
                share = 1.0 / total
                base = base * share
                weight = weight * share
                pieces = [base.astype(jnp.bfloat16)]
                for chain in range(chains):
                    pieces.append(
                        (weight * state[(chain + 1) * scn : (chain + 2) * scn, :]).astype(jnp.bfloat16)
                    )
                pieces.append((base * level).astype(jnp.bfloat16))
                moved = jnp.dot(
                    jnp.concatenate(pieces, axis=0), table[...], preferred_element_type=jnp.float32
                )
                state[: (chains + 2) * scn, :] = moved
            else:
                for at in range(hours):
                    if at == 0:
                        marked = base * level
                    else:
                        chain = hours - 1 - at
                        marked = weight * state[(chain + 1) * scn : (chain + 2) * scn, :]
                    mean = jnp.sum(marked, axis=-1, keepdims=True) / total
                    here = lane == (at % per_row) * gens + slot
                    outs[at // per_row] = jnp.where(here, mean, outs[at // per_row])
    for slot in range(gens):
        here = lane == (hours % per_row) * gens + slot
        bus = jnp.sum(jnp.where(lane == slot, bus_row, 0)).astype(jnp.float32)
        outs[-1] = jnp.where(here, bus, outs[-1])
    for part in range(parts):
        for row, block in enumerate(outs):
            out_ref[part, row] = block[part * scn_dev : (part + 1) * scn_dev, :]
    for copy in copies[6:]:
        copy.wait()


def run_plan(counts, gen_bus, transitions, level, cost, bus_price, ahead, parts):
    hours, scn, _ = bus_price.shape
    gens = level.shape[0]
    big_total = BIG_GROUP * (gens // GROUP)
    rows = -(-hours // (LANES // gens))
    hbm = pl.BlockSpec(memory_space=pltpu.HBM)
    vmem = pl.BlockSpec(memory_space=pltpu.VMEM)
    return pl.pallas_call(
        functools.partial(plan_kernel, gens=gens, parts=parts),
        out_shape=(pltpu.VMEM((parts, rows, scn // parts, LANES), jnp.float32),)
        + tuple(pltpu.VMEM(array.shape, array.dtype) for array in ahead),
        in_specs=[hbm] * (6 + len(ahead)),
        out_specs=(vmem,) * (1 + len(ahead)),
        scratch_shapes=[
            pltpu.SMEM(counts.shape, jnp.int32),
            pltpu.SMEM(gen_bus.shape, jnp.int32),
            pltpu.VMEM(transitions.shape, jnp.int32),
            pltpu.VMEM(level.shape, jnp.float32),
            pltpu.VMEM(cost.shape, jnp.float32),
            pltpu.VMEM(bus_price.shape, jnp.float32),
            pltpu.SMEM((gens,), jnp.int32),
            pltpu.VMEM((gens, SUBLANES, STATES), jnp.float32),
            pltpu.VMEM((gens, SUBLANES, STATES), jnp.float32),
            pltpu.VMEM((hours, scn, LANES), jnp.float32),
            pltpu.VMEM((big_total, STATES, STATES), jnp.bfloat16),
            pltpu.VMEM((gens - big_total, HALF, HALF), jnp.bfloat16),
            pltpu.VMEM((big_total, (hours + 1) * scn, STATES), jnp.float32),
            pltpu.VMEM((gens - big_total, (hours + 1) * scn, HALF), jnp.float32),
            pltpu.SemaphoreType.DMA((6 + len(ahead),)),
        ],
        compiler_params=pltpu.CompilerParams(vmem_limit_bytes=32 * 2**20),
        name="plan",
    )(
        *(
            pltpu.with_memory_space_constraint(array, pltpu.HBM)
            for array in (counts, gen_bus, transitions, level, cost, bus_price) + ahead
        )
    )


def net_kernel(plan_ref, demand_ref, net_ref, *, gens):
    parts, rows, scn_dev, _ = plan_ref.shape
    hours, _, bus_dev = demand_ref.shape
    per_row = LANES // gens
    lane = lax.broadcasted_iota(jnp.int32, (1, LANES), 1)
    bus_ids = lax.broadcasted_iota(jnp.int32, (bus_dev, LANES), 0).astype(jnp.float32)

    def of_hour(hour):
        start = (hour % per_row) * gens
        return (lane >= start) & (lane < start + gens)

    left, places = [], []
    for part in range(parts):
        values = [plan_ref[part, row] for row in range(rows)]
        left.append(
            jnp.concatenate(
                [jnp.where(of_hour(hour), values[hour // per_row], 0.0) for hour in range(hours)], axis=0
            )
        )
        bus = jnp.where(of_hour(hours), values[-1][:1, :], 0.0)
        bus = jnp.broadcast_to(bus, (SUBLANES, LANES))
        shift = gens
        while shift < LANES:
            bus = bus + pltpu.roll(bus, shift, 1)
            shift *= 2
        places.append((bus_ids == bus[:1, :]).astype(jnp.bfloat16))
    left = jnp.concatenate(left, axis=1)
    high = left.astype(jnp.bfloat16)
    rest = left - high.astype(jnp.float32)
    middle = rest.astype(jnp.bfloat16)
    low = (rest - middle.astype(jnp.float32)).astype(jnp.bfloat16)
    placed = lax.dot_general(
        jnp.concatenate([high, middle, low], axis=0),
        jnp.concatenate(places, axis=1),
        (((1,), (1,)), ((), ())),
        preferred_element_type=jnp.float32,
    )
    count = left.shape[0]
    injections = placed[:count] + (placed[count : 2 * count] + placed[2 * count :])
    demand = jnp.concatenate([demand_ref[hour] for hour in range(hours)], axis=0)
    net_ref[...] = (injections - demand).astype(jnp.bfloat16)


def line_kernel(
    pattern_smem,
    place_smem,
    own_ref,
    *refs,
    half,
):
    net_refs, refs = (own_ref,) + refs[: 2 * half - 1], refs[2 * half - 1 :]
    blocks_ref, limits_ref, old_ref, price_hbm, new_ref, near_out, far_out = refs[:7]
    net_all, spread_all, price_ref, sem = refs[7:]
    price_copy = pltpu.make_async_copy(price_hbm, price_ref, sem)
    price_copy.start()
    line_blocks, branches = pattern_smem.shape
    _, hours, scn_dev, _ = old_ref.shape
    row_total, bus_dev = own_ref.shape
    per_dev = bus_dev // BLK
    me = place_smem[0]
    my_pair, my_side = me // 2, lax.rem(me, 2)

    for at, net_ref in enumerate(net_refs):
        net_all[at] = net_ref[...]
    spread_all[...] = jnp.zeros(spread_all.shape, jnp.float32)

    def spot(line, branch):
        block = pattern_smem[line, branch]
        owner = block // per_dev
        column = pl.multiple_of(lax.rem(block, per_dev) * BLK, BLK)
        step = lax.rem(my_pair - owner // 2 + half, half)
        side = jnp.where(lax.rem(owner, 2) == my_side, 0, half)
        return side + step, column

    for line in range(line_blocks):
        spots = [spot(line, branch) for branch in range(branches)]
        picked = [net_all[at, :, pl.ds(column, BLK)] for at, column in spots]
        table = blocks_ref[line].reshape(branches * BLK, BLK)
        flow = jnp.dot(
            jnp.concatenate(picked, axis=1), table, preferred_element_type=jnp.float32
        )
        lanes = pl.ds(line * BLK, BLK)
        limit = limits_ref[lanes].reshape(1, BLK)
        upper_old = jnp.concatenate([old_ref[0, hour, :, lanes] for hour in range(hours)], axis=0)
        lower_old = jnp.concatenate([old_ref[1, hour, :, lanes] for hour in range(hours)], axis=0)
        upper = jnp.maximum(0.0, upper_old + (flow - limit))
        lower = jnp.maximum(0.0, lower_old + (-flow - limit))
        for hour in range(hours):
            here = slice(hour * scn_dev, (hour + 1) * scn_dev)
            new_ref[0, hour, :, lanes] = upper[here]
            new_ref[1, hour, :, lanes] = lower[here]
        change = ((upper - upper_old) - (lower - lower_old)).astype(jnp.bfloat16)
        spread = lax.dot_general(
            change, table, (((1,), (1,)), ((), ())), preferred_element_type=jnp.float32
        )
        for branch, (at, column) in enumerate(spots):
            spread_all[at, :, pl.ds(column, BLK)] += spread[:, branch * BLK : (branch + 1) * BLK]
    far_out[...] = spread_all[half:].astype(jnp.bfloat16)
    near_out[...] = spread_all[:half]
    price_copy.wait()
    part = place_smem[1]
    for hour in range(hours):
        price = price_ref[hour, :scn_dev, :]
        for other in range(1, price_ref.shape[1] // scn_dev):
            price = jnp.where(part == other, price_ref[hour, other * scn_dev : (other + 1) * scn_dev, :], price)
        here = slice(hour * scn_dev, (hour + 1) * scn_dev)
        near_out[0, here, :] = spread_all[0, here, :] - price


def price_kernel(place_smem, *refs):
    share_refs, (out_ref, share_all) = refs[:-2], refs[-2:]
    hours = out_ref.shape[0]
    parts = len(share_refs)
    scn_dev = out_ref.shape[1] // parts
    me = place_smem[1]
    for step, share in enumerate(share_refs):
        share_all[step] = share[...]
    steps = [lax.rem(me - part + parts, parts) for part in range(parts)]
    for hour in range(hours):
        less = [share_all[step, hour * scn_dev : (hour + 1) * scn_dev, :] for step in steps]
        out_ref[hour] = -jnp.concatenate(less, axis=0)


def shards(
    bus_price,
    bus_demand,
    multipliers,
    line_limits,
    ptdf_blocks,
    ptdf_pattern,
    gen_bus,
    state_counts,
    transitions,
    state_level,
    state_cost,
):
    scn_dev, hours, bus_dev = bus_demand.shape
    parts = lax.axis_size("gen")
    ring = lax.axis_size("bus")
    half = ring // 2
    gens = state_level.shape[0]
    row_total = scn_dev * hours
    place = jnp.stack([lax.axis_index("bus"), lax.axis_index("gen")]).astype(jnp.int32)
    smem = pl.BlockSpec(memory_space=pltpu.SMEM)
    vmem = pl.BlockSpec(memory_space=pltpu.VMEM)
    roomy = pltpu.CompilerParams(vmem_limit_bytes=24 * 2**20)
    pairs = [(i, i ^ 1) for i in range(ring)]

    def shifted(step):
        return [(i, (i + 2 * step) % ring) for i in range(ring)]

    bus_price = jnp.transpose(bus_price, (1, 0, 2))
    bus_demand = jnp.transpose(bus_demand, (1, 0, 2))
    multipliers = jnp.transpose(multipliers, (0, 2, 1, 3))
    transitions = jnp.transpose(transitions, (1, 0, 2))
    ahead = (bus_demand, ptdf_blocks, multipliers, line_limits, ptdf_pattern)
    plan, *ahead = run_plan(
        state_counts, gen_bus, transitions, state_level, state_cost, bus_price, ahead, parts
    )
    bus_demand, ptdf_blocks, multipliers, line_limits, ptdf_pattern = ahead
    received = lax.all_to_all(plan, "gen", split_axis=0, concat_axis=0, tiled=True)
    net = pl.pallas_call(
        functools.partial(net_kernel, gens=gens),
        out_shape=jax.ShapeDtypeStruct((row_total, bus_dev), jnp.bfloat16),
        in_specs=[vmem, vmem],
        out_specs=vmem,
        compiler_params=roomy,
        name="net",
    )(received, bus_demand)

    far = [lax.ppermute(net, "bus", shifted(step)) for step in range(1, half)]
    other = [lax.ppermute(piece, "bus", pairs) for piece in [net] + far]
    new_multipliers, near_part, far_part = pl.pallas_call(
        functools.partial(line_kernel, half=half),
        out_shape=(
            jax.ShapeDtypeStruct(multipliers.shape, jnp.float32),
            jax.ShapeDtypeStruct((half, row_total, bus_dev), jnp.float32),
            jax.ShapeDtypeStruct((half, row_total, bus_dev), jnp.bfloat16),
        ),
        in_specs=[smem, smem] + [vmem] * (ring + 3) + [pl.BlockSpec(memory_space=pltpu.HBM)],
        out_specs=(vmem, vmem, vmem),
        scratch_shapes=[
            pltpu.VMEM((ring, row_total, bus_dev), jnp.bfloat16),
            pltpu.VMEM((ring, row_total, bus_dev), jnp.float32),
            pltpu.VMEM(bus_price.shape, jnp.float32),
            pltpu.SemaphoreType.DMA,
        ],
        compiler_params=roomy,
        name="lines",
    )(
        ptdf_pattern,
        place,
        net,
        *far,
        *other,
        ptdf_blocks,
        line_limits,
        multipliers,
        pltpu.with_memory_space_constraint(bus_price, pltpu.HBM),
    )

    traded = lax.ppermute(far_part, "bus", pairs)
    own_change = near_part[0] + traded[0].astype(jnp.float32)
    for step in range(1, half):
        share = (near_part[step] + traded[step].astype(jnp.float32)).astype(jnp.bfloat16)
        own_change = own_change + lax.ppermute(share, "bus", shifted(half - step)).astype(jnp.float32)
    shares = [own_change] + [
        lax.ppermute(own_change, "gen", [(i, (i + step) % parts) for i in range(parts)])
        for step in range(1, parts)
    ]
    new_price = pl.pallas_call(
        price_kernel,
        out_shape=jax.ShapeDtypeStruct(bus_price.shape, jnp.float32),
        in_specs=[smem] + [vmem] * parts,
        out_specs=vmem,
        scratch_shapes=[pltpu.VMEM((parts, row_total, bus_dev), jnp.float32)],
        compiler_params=roomy,
        name="price",
    )(place, *shares)
    return (jnp.transpose(new_multipliers, (0, 2, 1, 3)), jnp.transpose(new_price, (1, 0, 2)))


def solution(mesh):
    in_specs = (
        P(None, None, "bus"),
        P("gen", None, "bus"),
        P(None, "gen", None, "bus"),
        P("bus"),
        P("bus", None, None, None),
        P("bus", None),
        P(("gen", "bus")),
        P(("gen", "bus")),
        P(("gen", "bus"), None, None),
        P(("gen", "bus"), None),
        P(("gen", "bus"), None),
    )
    out_specs = (P(None, "gen", None, "bus"), P(None, None, "bus"))
    return jax.shard_map(shards, mesh=mesh, in_specs=in_specs, out_specs=out_specs, check_vma=False)
```

```python
import functools

import jax
import jax.numpy as jnp
from jax import lax
from jax.experimental import pallas as pl
from jax.experimental.pallas import tpu as pltpu
from jax.sharding import PartitionSpec as P

STATES = 512
HALF = 256
BLK = 128
NNZB = 16
GROUP = 16
BIG_GROUP = 6
LANES = 128
AHEAD = 5
SUBLANES = 8
EXACT = lax.Precision.HIGHEST


def plan_kernel(*refs, gens, parts):
    (counts_hbm, bus_hbm, trans_hbm, level_hbm, cost_hbm, price_hbm), refs = refs[:6], refs[6:]
    ahead_hbm, refs = refs[:AHEAD], refs[AHEAD:]
    out_ref, refs = refs[0], refs[1:]
    ahead_refs, refs = refs[:AHEAD], refs[AHEAD:]
    (
        counts_smem,
        bus_smem,
        trans_ref,
        level_ref,
        cost_ref,
        price_ref,
        order,
        level_slot,
        cost_slot,
        gen_price,
        big_table,
        small_table,
        big_state,
        small_state,
        sems,
    ) = refs
    sources = (counts_hbm, bus_hbm, trans_hbm, level_hbm, cost_hbm, price_hbm) + ahead_hbm
    targets = (counts_smem, bus_smem, trans_ref, level_ref, cost_ref, price_ref) + ahead_refs
    copies = [
        pltpu.make_async_copy(source, target, sems.at[at])
        for at, (source, target) in enumerate(zip(sources, targets))
    ]
    for copy in copies:
        copy.start()
    hours, scn, bus_dev = price_ref.shape
    big_total = BIG_GROUP * (gens // GROUP)
    scn_dev = scn // parts
    per_row = LANES // gens
    for copy in copies[:2]:
        copy.wait()

    def place(gen, taken):
        big = (counts_smem[gen] > HALF).astype(jnp.int32)
        slot = jnp.where(big == 1, taken, gens - 1 - (gen - taken))
        order[slot] = gen
        return taken + big

    lax.fori_loop(0, gens, place, jnp.int32(0))

    for copy in copies[2:6]:
        copy.wait()
    lane = lax.broadcasted_iota(jnp.int32, (1, LANES), 1)
    local_row = jnp.zeros((1, LANES), jnp.int32)
    bus_row = jnp.zeros((1, LANES), jnp.int32)
    for slot in range(gens):
        local = lax.rem(bus_smem[order[slot]], bus_dev)
        local_row = jnp.where(lane == slot, local, local_row)
        bus_row = jnp.where(lane == slot, local, bus_row)
    chooser = (
        lax.broadcasted_iota(jnp.int32, (bus_dev, LANES), 0) == local_row
    ).astype(jnp.float32)
    for hour in range(hours):
        gen_price[hour] = lax.dot_general(
            price_ref[hour],
            chooser,
            (((1,), (0,)), ((), ())),
            precision=EXACT,
            preferred_element_type=jnp.float32,
        )

    state_ids = lax.broadcasted_iota(jnp.int32, (1, STATES), 1)
    spans = []
    for slot in range(gens):
        gen = order[slot]
        span = STATES if slot < big_total else HALF
        spans.append(span)
        level_slot[slot] = jnp.broadcast_to(level_ref[pl.ds(gen, 1), :], (SUBLANES, STATES))
        cost_row = jnp.where(state_ids < counts_smem[gen], cost_ref[pl.ds(gen, 1), :], 1e30)
        cost_slot[slot] = jnp.broadcast_to(cost_row, (SUBLANES, STATES))
        successors = [trans_ref[branch, pl.ds(gen, 1), :] for branch in range(trans_ref.shape[0])]
        table = big_table.at[slot] if slot < big_total else small_table.at[slot - big_total]
        for first in range(0, span, HALF):
            rows = lax.broadcasted_iota(jnp.int32, (HALF, span), 0).astype(jnp.float32).astype(jnp.bfloat16)
            one = jnp.ones((HALF, span), jnp.bfloat16)
            none = jnp.zeros((HALF, span), jnp.bfloat16)
            total = none
            for row in successors:
                shifted = (row[:, :span] - first).astype(jnp.float32).astype(jnp.bfloat16)
                total = total + jnp.where(rows == shifted, one, none)
            table[pl.ds(first, HALF), :] = total

    def repeat_rows(block, copies):
        return block if copies == 1 else jnp.concatenate([block] * copies, axis=0)

    outs = [jnp.zeros((scn, LANES), jnp.float32) for _ in range(-(-hours // per_row))]
    for hour in range(hours - 1, -1, -1):
        chains = hours - 1 - hour
        for slot in range(gens):
            span = spans[slot]
            if slot < big_total:
                state, table = big_state.at[slot], big_table.at[slot]
            else:
                state, table = small_state.at[slot - big_total], small_table.at[slot - big_total]
            level = repeat_rows(level_slot[slot][:, :span], scn // SUBLANES)
            cost = repeat_rows(cost_slot[slot][:, :span], scn // SUBLANES)
            price = gen_price[hour][:, slot : slot + 1]
            weight = jnp.exp(price * level - cost)
            base = weight if chains == 0 else weight * state[:scn, :]
            total = jnp.sum(base, axis=-1, keepdims=True)
            if hour > 0:
                share = 1.0 / total
                base = base * share
                weight = weight * share
                pieces = [base.astype(jnp.bfloat16)]
                for chain in range(chains):
                    pieces.append(
                        (weight * state[(chain + 1) * scn : (chain + 2) * scn, :]).astype(jnp.bfloat16)
                    )
                pieces.append((base * level).astype(jnp.bfloat16))
                moved = jnp.dot(
                    jnp.concatenate(pieces, axis=0), table[...], preferred_element_type=jnp.float32
                )
                state[: (chains + 2) * scn, :] = moved
            else:
                for at in range(hours):
                    if at == 0:
                        marked = base * level
                    else:
                        chain = hours - 1 - at
                        marked = weight * state[(chain + 1) * scn : (chain + 2) * scn, :]
                    mean = jnp.sum(marked, axis=-1, keepdims=True) / total
                    here = lane == (at % per_row) * gens + slot
                    outs[at // per_row] = jnp.where(here, mean, outs[at // per_row])
    for slot in range(gens):
        here = lane == (hours % per_row) * gens + slot
        bus = jnp.sum(jnp.where(lane == slot, bus_row, 0)).astype(jnp.float32)
        outs[-1] = jnp.where(here, bus, outs[-1])
    for part in range(parts):
        for row, block in enumerate(outs):
            out_ref[part, row] = block[part * scn_dev : (part + 1) * scn_dev, :]
    for copy in copies[6:]:
        copy.wait()


def run_plan(counts, gen_bus, transitions, level, cost, bus_price, ahead, parts):
    hours, scn, _ = bus_price.shape
    gens = level.shape[0]
    big_total = BIG_GROUP * (gens // GROUP)
    rows = -(-hours // (LANES // gens))
    hbm = pl.BlockSpec(memory_space=pltpu.HBM)
    vmem = pl.BlockSpec(memory_space=pltpu.VMEM)
    return pl.pallas_call(
        functools.partial(plan_kernel, gens=gens, parts=parts),
        out_shape=(pltpu.VMEM((parts, rows, scn // parts, LANES), jnp.float32),)
        + tuple(pltpu.VMEM(array.shape, array.dtype) for array in ahead),
        in_specs=[hbm] * (6 + len(ahead)),
        out_specs=(vmem,) * (1 + len(ahead)),
        scratch_shapes=[
            pltpu.SMEM(counts.shape, jnp.int32),
            pltpu.SMEM(gen_bus.shape, jnp.int32),
            pltpu.VMEM(transitions.shape, jnp.int32),
            pltpu.VMEM(level.shape, jnp.float32),
            pltpu.VMEM(cost.shape, jnp.float32),
            pltpu.VMEM(bus_price.shape, jnp.float32),
            pltpu.SMEM((gens,), jnp.int32),
            pltpu.VMEM((gens, SUBLANES, STATES), jnp.float32),
            pltpu.VMEM((gens, SUBLANES, STATES), jnp.float32),
            pltpu.VMEM((hours, scn, LANES), jnp.float32),
            pltpu.VMEM((big_total, STATES, STATES), jnp.bfloat16),
            pltpu.VMEM((gens - big_total, HALF, HALF), jnp.bfloat16),
            pltpu.VMEM((big_total, (hours + 1) * scn, STATES), jnp.float32),
            pltpu.VMEM((gens - big_total, (hours + 1) * scn, HALF), jnp.float32),
            pltpu.SemaphoreType.DMA((6 + len(ahead),)),
        ],
        compiler_params=pltpu.CompilerParams(vmem_limit_bytes=32 * 2**20),
        name="plan",
    )(
        *(
            pltpu.with_memory_space_constraint(array, pltpu.HBM)
            for array in (counts, gen_bus, transitions, level, cost, bus_price) + ahead
        )
    )


def net_kernel(plan_ref, demand_ref, net_ref, *, gens):
    parts, rows, scn_dev, _ = plan_ref.shape
    hours, _, bus_dev = demand_ref.shape
    per_row = LANES // gens
    lane = lax.broadcasted_iota(jnp.int32, (1, LANES), 1)
    bus_ids = lax.broadcasted_iota(jnp.int32, (bus_dev, LANES), 0).astype(jnp.float32)

    def of_hour(hour):
        start = (hour % per_row) * gens
        return (lane >= start) & (lane < start + gens)

    left, places = [], []
    for part in range(parts):
        values = [plan_ref[part, row] for row in range(rows)]
        left.append(
            jnp.concatenate(
                [jnp.where(of_hour(hour), values[hour // per_row], 0.0) for hour in range(hours)], axis=0
            )
        )
        bus = jnp.where(of_hour(hours), values[-1][:1, :], 0.0)
        bus = jnp.broadcast_to(bus, (SUBLANES, LANES))
        shift = gens
        while shift < LANES:
            bus = bus + pltpu.roll(bus, shift, 1)
            shift *= 2
        places.append((bus_ids == bus[:1, :]).astype(jnp.bfloat16))
    left = jnp.concatenate(left, axis=1)
    high = left.astype(jnp.bfloat16)
    rest = left - high.astype(jnp.float32)
    middle = rest.astype(jnp.bfloat16)
    low = (rest - middle.astype(jnp.float32)).astype(jnp.bfloat16)
    placed = lax.dot_general(
        jnp.concatenate([high, middle, low], axis=0),
        jnp.concatenate(places, axis=1),
        (((1,), (1,)), ((), ())),
        preferred_element_type=jnp.float32,
    )
    count = left.shape[0]
    injections = placed[:count] + (placed[count : 2 * count] + placed[2 * count :])
    demand = jnp.concatenate([demand_ref[hour] for hour in range(hours)], axis=0)
    net_ref[...] = (injections - demand).astype(jnp.bfloat16)


def line_kernel(pattern_smem, *refs, half):
    net_refs, refs = refs[: 2 * half], refs[2 * half :]
    blocks_ref, limits_ref, old_ref, price_hbm, new_hbm, spread_all, far_out = refs[:7]
    net_all, new_ref, price_ref, sems = refs[7:]
    price_copy = pltpu.make_async_copy(price_hbm, price_ref, sems.at[0])
    price_copy.start()
    new_copy = pltpu.make_async_copy(new_ref, new_hbm, sems.at[1])
    line_blocks, branches = pattern_smem.shape
    _, hours, scn_dev, _ = old_ref.shape
    bus_dev = net_refs[0].shape[1]
    per_dev = bus_dev // BLK
    me = lax.axis_index("bus")
    my_pair, my_side = me // 2, lax.rem(me, 2)

    for at, net_ref in enumerate(net_refs):
        net_all[at] = net_ref[...]
    spread_all[...] = jnp.zeros(spread_all.shape, jnp.float32)

    def spot(line, branch):
        block = pattern_smem[line, branch]
        owner = block // per_dev
        column = pl.multiple_of(lax.rem(block, per_dev) * BLK, BLK)
        step = lax.bitwise_xor(my_pair, owner // 2)
        side = jnp.where(lax.rem(owner, 2) == my_side, 0, half)
        return side + step, column

    spots = [[spot(line, branch) for branch in range(branches)] for line in range(line_blocks)]
    tables = [blocks_ref.at[line] for line in range(line_blocks)]
    changes = []
    for line in range(line_blocks):
        picked = [net_all[at, :, pl.ds(column, BLK)] for at, column in spots[line]]
        flow = jnp.dot(
            jnp.concatenate(picked, axis=1),
            tables[line][...].reshape(branches * BLK, BLK),
            preferred_element_type=jnp.float32,
        )
        lanes = pl.ds(line * BLK, BLK)
        limit = limits_ref[lanes].reshape(1, BLK)
        upper_old = jnp.concatenate([old_ref[0, hour, :, lanes] for hour in range(hours)], axis=0)
        lower_old = jnp.concatenate([old_ref[1, hour, :, lanes] for hour in range(hours)], axis=0)
        upper = jnp.maximum(0.0, upper_old + (flow - limit))
        lower = jnp.maximum(0.0, lower_old + (-flow - limit))
        for hour in range(hours):
            here = slice(hour * scn_dev, (hour + 1) * scn_dev)
            new_ref[0, hour, :, lanes] = upper[here]
            new_ref[1, hour, :, lanes] = lower[here]
        changes.append(((upper - upper_old) - (lower - lower_old)).astype(jnp.bfloat16))
    new_copy.start()
    for line in range(line_blocks):
        spread = lax.dot_general(
            changes[line],
            tables[line][...].reshape(branches * BLK, BLK),
            (((1,), (1,)), ((), ())),
            preferred_element_type=jnp.float32,
        )
        held = [spread_all[at, :, pl.ds(column, BLK)] for at, column in spots[line]]
        for branch, (at, column) in enumerate(spots[line]):
            spread_all[at, :, pl.ds(column, BLK)] = (
                held[branch] + spread[:, branch * BLK : (branch + 1) * BLK]
            )
    far_out[...] = spread_all[half:].astype(jnp.bfloat16)
    price_copy.wait()
    part = lax.axis_index("gen")
    for hour in range(hours):
        price = price_ref[hour, :scn_dev, :]
        for other in range(1, price_ref.shape[1] // scn_dev):
            price = jnp.where(part == other, price_ref[hour, other * scn_dev : (other + 1) * scn_dev, :], price)
        here = slice(hour * scn_dev, (hour + 1) * scn_dev)
        spread_all[0, here, :] = spread_all[0, here, :] - price
    new_copy.wait()


def run_lines(pattern, nets, blocks, limits, old, bus_price):
    ring = len(nets)
    half = ring // 2
    smem = pl.BlockSpec(memory_space=pltpu.SMEM)
    vmem = pl.BlockSpec(memory_space=pltpu.VMEM)
    hbm = pl.BlockSpec(memory_space=pltpu.HBM)
    return pl.pallas_call(
        functools.partial(line_kernel, half=half),
        out_shape=(
            jax.ShapeDtypeStruct(old.shape, jnp.float32),
            jax.ShapeDtypeStruct((ring,) + nets[0].shape, jnp.float32),
            jax.ShapeDtypeStruct((half,) + nets[0].shape, jnp.bfloat16),
        ),
        in_specs=[smem] + [vmem] * (ring + 3) + [hbm],
        out_specs=(hbm, vmem, vmem),
        scratch_shapes=[
            pltpu.VMEM((ring,) + nets[0].shape, jnp.bfloat16),
            pltpu.VMEM(old.shape, jnp.float32),
            pltpu.VMEM(bus_price.shape, jnp.float32),
            pltpu.SemaphoreType.DMA((2,)),
        ],
        compiler_params=pltpu.CompilerParams(vmem_limit_bytes=24 * 2**20),
        name="lines",
    )(
        pattern,
        *nets,
        blocks,
        limits,
        old,
        pltpu.with_memory_space_constraint(bus_price, pltpu.HBM),
    )


def price_kernel(*refs):
    share_refs, (out_ref, share_all) = refs[:-2], refs[-2:]
    hours = out_ref.shape[0]
    parts = len(share_refs)
    scn_dev = out_ref.shape[1] // parts
    me = lax.axis_index("gen")
    for step, share in enumerate(share_refs):
        share_all[step] = share[...]
    steps = [lax.bitwise_xor(me, part) for part in range(parts)]
    for hour in range(hours):
        less = [share_all[step, hour * scn_dev : (hour + 1) * scn_dev, :] for step in steps]
        out_ref[hour] = -jnp.concatenate(less, axis=0)


def shards(
    bus_price,
    bus_demand,
    multipliers,
    line_limits,
    ptdf_blocks,
    ptdf_pattern,
    gen_bus,
    state_counts,
    transitions,
    state_level,
    state_cost,
):
    scn_dev, hours, bus_dev = bus_demand.shape
    parts = lax.axis_size("gen")
    ring = lax.axis_size("bus")
    half = ring // 2
    gens = state_level.shape[0]
    row_total = scn_dev * hours
    vmem = pl.BlockSpec(memory_space=pltpu.VMEM)
    roomy = pltpu.CompilerParams(vmem_limit_bytes=24 * 2**20)

    def trade(size, step):
        return [(i, i ^ step) for i in range(size)]

    bus_price = jnp.transpose(bus_price, (1, 0, 2))
    bus_demand = jnp.transpose(bus_demand, (1, 0, 2))
    multipliers = jnp.transpose(multipliers, (0, 2, 1, 3))
    transitions = jnp.transpose(transitions, (1, 0, 2))
    ahead = (bus_demand, ptdf_blocks, multipliers, line_limits, ptdf_pattern)
    plan, *ahead = run_plan(
        state_counts, gen_bus, transitions, state_level, state_cost, bus_price, ahead, parts
    )
    bus_demand, ptdf_blocks, multipliers, line_limits, ptdf_pattern = ahead
    received = lax.all_to_all(plan, "gen", split_axis=0, concat_axis=0, tiled=True)
    net = pl.pallas_call(
        functools.partial(net_kernel, gens=gens),
        out_shape=jax.ShapeDtypeStruct((row_total, bus_dev), jnp.bfloat16),
        in_specs=[vmem, vmem],
        out_specs=vmem,
        compiler_params=roomy,
        name="net",
    )(received, bus_demand)

    far = [lax.ppermute(net, "bus", trade(ring, 2 * step)) for step in range(1, half)]
    other = [lax.ppermute(piece, "bus", trade(ring, 1)) for piece in [net] + far]
    new_multipliers, spread, far_part = run_lines(
        ptdf_pattern, [net] + far + other, ptdf_blocks, line_limits, multipliers, bus_price
    )

    traded = [lax.ppermute(far_part[step], "bus", trade(ring, 1)).astype(jnp.float32) for step in range(half)]
    own_change = spread[0] + traded[0]
    for step in range(1, half):
        share = (spread[step] + traded[step]).astype(jnp.bfloat16)
        own_change = own_change + lax.ppermute(share, "bus", trade(ring, 2 * step)).astype(jnp.float32)
    shares = [own_change]
    for step in range(1, parts):
        moved, by = (shares[step - 1], 1) if step % 2 else (own_change, step)
        shares.append(lax.ppermute(moved, "gen", trade(parts, by)))
    new_price = pl.pallas_call(
        price_kernel,
        out_shape=jax.ShapeDtypeStruct(bus_price.shape, jnp.float32),
        in_specs=[vmem] * parts,
        out_specs=vmem,
        scratch_shapes=[pltpu.VMEM((parts, row_total, bus_dev), jnp.float32)],
        compiler_params=roomy,
        name="price",
    )(*shares)
    return (jnp.transpose(new_multipliers, (0, 2, 1, 3)), jnp.transpose(new_price, (1, 0, 2)))


def solution(mesh):
    in_specs = (
        P(None, None, "bus"),
        P("gen", None, "bus"),
        P(None, "gen", None, "bus"),
        P("bus"),
        P("bus", None, None, None),
        P("bus", None),
        P(("gen", "bus")),
        P(("gen", "bus")),
        P(("gen", "bus"), None, None),
        P(("gen", "bus"), None),
        P(("gen", "bus"), None),
    )
    out_specs = (P(None, "gen", None, "bus"), P(None, None, "bus"))
    return jax.shard_map(shards, mesh=mesh, in_specs=in_specs, out_specs=out_specs, check_vma=False)
```

```python
import functools

import jax
import jax.numpy as jnp
from jax import lax
from jax.experimental import pallas as pl
from jax.experimental.pallas import tpu as pltpu
from jax.sharding import PartitionSpec as P

STATES = 512
HALF = 256
BLK = 128
NNZB = 16
GROUP = 16
BIG_GROUP = 6
LANES = 128
AHEAD = 5
DIRECT = 1
SUBLANES = 8
EXACT = lax.Precision.HIGHEST


def plan_kernel(*refs, gens, parts):
    (counts_hbm, bus_hbm, trans_hbm, level_hbm, cost_hbm, price_hbm), refs = refs[:6], refs[6:]
    ahead_hbm, refs = refs[:AHEAD], refs[AHEAD:]
    out_ref, refs = refs[0], refs[1:]
    ahead_refs, refs = refs[:AHEAD], refs[AHEAD:]
    (
        counts_smem,
        bus_smem,
        trans_ref,
        level_ref,
        cost_ref,
        price_ref,
        order,
        level_slot,
        cost_slot,
        gen_price,
        big_table,
        small_table,
        big_state,
        small_state,
        sems,
    ) = refs
    sources = (counts_hbm, bus_hbm, trans_hbm, level_hbm, cost_hbm, price_hbm) + ahead_hbm
    targets = (counts_smem, bus_smem, trans_ref, level_ref, cost_ref, price_ref) + ahead_refs
    copies = [
        pltpu.make_async_copy(source, target, sems.at[at])
        for at, (source, target) in enumerate(zip(sources, targets))
    ]
    for copy in copies:
        copy.start()
    hours, scn, bus_dev = price_ref.shape
    big_total = BIG_GROUP * (gens // GROUP)
    scn_dev = scn // parts
    per_row = LANES // gens
    for copy in copies[:2]:
        copy.wait()

    def place(gen, taken):
        big = (counts_smem[gen] > HALF).astype(jnp.int32)
        slot = jnp.where(big == 1, taken, gens - 1 - (gen - taken))
        order[slot] = gen
        return taken + big

    lax.fori_loop(0, gens, place, jnp.int32(0))

    for copy in copies[2:6]:
        copy.wait()
    lane = lax.broadcasted_iota(jnp.int32, (1, LANES), 1)
    local_row = jnp.zeros((1, LANES), jnp.int32)
    bus_row = jnp.zeros((1, LANES), jnp.int32)
    for slot in range(gens):
        local = lax.rem(bus_smem[order[slot]], bus_dev)
        local_row = jnp.where(lane == slot, local, local_row)
        bus_row = jnp.where(lane == slot, local, bus_row)
    chooser = (
        lax.broadcasted_iota(jnp.int32, (bus_dev, LANES), 0) == local_row
    ).astype(jnp.float32)
    for hour in range(hours):
        gen_price[hour] = lax.dot_general(
            price_ref[hour],
            chooser,
            (((1,), (0,)), ((), ())),
            precision=EXACT,
            preferred_element_type=jnp.float32,
        )

    state_ids = lax.broadcasted_iota(jnp.int32, (1, STATES), 1)
    spans = []
    for slot in range(gens):
        gen = order[slot]
        span = STATES if slot < big_total else HALF
        spans.append(span)
        level_slot[slot] = jnp.broadcast_to(level_ref[pl.ds(gen, 1), :], (SUBLANES, STATES))
        cost_row = jnp.where(state_ids < counts_smem[gen], cost_ref[pl.ds(gen, 1), :], 1e30)
        cost_slot[slot] = jnp.broadcast_to(cost_row, (SUBLANES, STATES))
        successors = [trans_ref[branch, pl.ds(gen, 1), :] for branch in range(trans_ref.shape[0])]
        table = big_table.at[slot] if slot < big_total else small_table.at[slot - big_total]
        for first in range(0, span, HALF):
            rows = lax.broadcasted_iota(jnp.int32, (HALF, span), 0).astype(jnp.float32).astype(jnp.bfloat16)
            one = jnp.ones((HALF, span), jnp.bfloat16)
            none = jnp.zeros((HALF, span), jnp.bfloat16)
            total = none
            for row in successors:
                shifted = (row[:, :span] - first).astype(jnp.float32).astype(jnp.bfloat16)
                total = total + jnp.where(rows == shifted, one, none)
            table[pl.ds(first, HALF), :] = total

    def repeat_rows(block, copies):
        return block if copies == 1 else jnp.concatenate([block] * copies, axis=0)

    outs = [jnp.zeros((scn, LANES), jnp.float32) for _ in range(-(-hours // per_row))]
    for hour in range(hours - 1, -1, -1):
        chains = hours - 1 - hour
        for slot in range(gens):
            span = spans[slot]
            if slot < big_total:
                state, table = big_state.at[slot], big_table.at[slot]
            else:
                state, table = small_state.at[slot - big_total], small_table.at[slot - big_total]
            level = repeat_rows(level_slot[slot][:, :span], scn // SUBLANES)
            cost = repeat_rows(cost_slot[slot][:, :span], scn // SUBLANES)
            price = gen_price[hour][:, slot : slot + 1]
            weight = jnp.exp(price * level - cost)
            base = weight if chains == 0 else weight * state[:scn, :]
            total = jnp.sum(base, axis=-1, keepdims=True)
            if hour > 0:
                share = 1.0 / total
                base = base * share
                weight = weight * share
                pieces = [base.astype(jnp.bfloat16)]
                for chain in range(chains):
                    pieces.append(
                        (weight * state[(chain + 1) * scn : (chain + 2) * scn, :]).astype(jnp.bfloat16)
                    )
                pieces.append((base * level).astype(jnp.bfloat16))
                moved = jnp.dot(
                    jnp.concatenate(pieces, axis=0), table[...], preferred_element_type=jnp.float32
                )
                state[: (chains + 2) * scn, :] = moved
            else:
                for at in range(hours):
                    if at == 0:
                        marked = base * level
                    else:
                        chain = hours - 1 - at
                        marked = weight * state[(chain + 1) * scn : (chain + 2) * scn, :]
                    mean = jnp.sum(marked, axis=-1, keepdims=True) / total
                    here = lane == (at % per_row) * gens + slot
                    outs[at // per_row] = jnp.where(here, mean, outs[at // per_row])
    for slot in range(gens):
        here = lane == (hours % per_row) * gens + slot
        bus = jnp.sum(jnp.where(lane == slot, bus_row, 0)).astype(jnp.float32)
        outs[-1] = jnp.where(here, bus, outs[-1])
    for part in range(parts):
        for row, block in enumerate(outs):
            out_ref[part, row] = block[part * scn_dev : (part + 1) * scn_dev, :]
    for copy in copies[6:]:
        copy.wait()


def run_plan(counts, gen_bus, transitions, level, cost, bus_price, ahead, parts):
    hours, scn, _ = bus_price.shape
    gens = level.shape[0]
    big_total = BIG_GROUP * (gens // GROUP)
    rows = -(-hours // (LANES // gens))
    hbm = pl.BlockSpec(memory_space=pltpu.HBM)
    vmem = pl.BlockSpec(memory_space=pltpu.VMEM)
    return pl.pallas_call(
        functools.partial(plan_kernel, gens=gens, parts=parts),
        out_shape=(pltpu.VMEM((parts, rows, scn // parts, LANES), jnp.float32),)
        + tuple(pltpu.VMEM(array.shape, array.dtype) for array in ahead),
        in_specs=[hbm] * (6 + len(ahead)),
        out_specs=(vmem,) * (1 + len(ahead)),
        scratch_shapes=[
            pltpu.SMEM(counts.shape, jnp.int32),
            pltpu.SMEM(gen_bus.shape, jnp.int32),
            pltpu.VMEM(transitions.shape, jnp.int32),
            pltpu.VMEM(level.shape, jnp.float32),
            pltpu.VMEM(cost.shape, jnp.float32),
            pltpu.VMEM(bus_price.shape, jnp.float32),
            pltpu.SMEM((gens,), jnp.int32),
            pltpu.VMEM((gens, SUBLANES, STATES), jnp.float32),
            pltpu.VMEM((gens, SUBLANES, STATES), jnp.float32),
            pltpu.VMEM((hours, scn, LANES), jnp.float32),
            pltpu.VMEM((big_total, STATES, STATES), jnp.bfloat16),
            pltpu.VMEM((gens - big_total, HALF, HALF), jnp.bfloat16),
            pltpu.VMEM((big_total, (hours + 1) * scn, STATES), jnp.float32),
            pltpu.VMEM((gens - big_total, (hours + 1) * scn, HALF), jnp.float32),
            pltpu.SemaphoreType.DMA((6 + len(ahead),)),
        ],
        compiler_params=pltpu.CompilerParams(vmem_limit_bytes=32 * 2**20),
        name="plan",
    )(
        *(
            pltpu.with_memory_space_constraint(array, pltpu.HBM)
            for array in (counts, gen_bus, transitions, level, cost, bus_price) + ahead
        )
    )


def net_kernel(plan_ref, demand_ref, net_ref, *, gens):
    parts, rows, scn_dev, _ = plan_ref.shape
    hours, _, bus_dev = demand_ref.shape
    per_row = LANES // gens
    lane = lax.broadcasted_iota(jnp.int32, (1, LANES), 1)
    bus_ids = lax.broadcasted_iota(jnp.int32, (bus_dev, LANES), 0).astype(jnp.float32)

    def of_hour(hour):
        start = (hour % per_row) * gens
        return (lane >= start) & (lane < start + gens)

    left, places = [], []
    for part in range(parts):
        values = [plan_ref[part, row] for row in range(rows)]
        left.append(
            jnp.concatenate(
                [jnp.where(of_hour(hour), values[hour // per_row], 0.0) for hour in range(hours)], axis=0
            )
        )
        bus = jnp.where(of_hour(hours), values[-1][:1, :], 0.0)
        bus = jnp.broadcast_to(bus, (SUBLANES, LANES))
        shift = gens
        while shift < LANES:
            bus = bus + pltpu.roll(bus, shift, 1)
            shift *= 2
        places.append((bus_ids == bus[:1, :]).astype(jnp.bfloat16))
    left = jnp.concatenate(left, axis=1)
    high = left.astype(jnp.bfloat16)
    rest = left - high.astype(jnp.float32)
    middle = rest.astype(jnp.bfloat16)
    low = (rest - middle.astype(jnp.float32)).astype(jnp.bfloat16)
    placed = lax.dot_general(
        jnp.concatenate([high, middle, low], axis=0),
        jnp.concatenate(places, axis=1),
        (((1,), (1,)), ((), ())),
        preferred_element_type=jnp.float32,
    )
    count = left.shape[0]
    injections = placed[:count] + (placed[count : 2 * count] + placed[2 * count :])
    demand = jnp.concatenate([demand_ref[hour] for hour in range(hours)], axis=0)
    net_ref[...] = (injections - demand).astype(jnp.bfloat16)


def line_kernel(pattern_smem, *refs, half):
    net_refs, refs = refs[: 2 * half], refs[2 * half :]
    blocks_ref, limits_ref, old_ref, price_hbm, new_hbm, spread_all, far_out = refs[:7]
    net_all, new_ref, price_ref, sems = refs[7:]
    price_copy = pltpu.make_async_copy(price_hbm, price_ref, sems.at[0])
    price_copy.start()
    new_copy = pltpu.make_async_copy(new_ref, new_hbm, sems.at[1])
    line_blocks, branches = pattern_smem.shape
    _, hours, scn_dev, _ = old_ref.shape
    bus_dev = net_refs[0].shape[1]
    per_dev = bus_dev // BLK
    me = lax.axis_index("bus")
    my_pair, my_side = me // 2, lax.rem(me, 2)

    for at, net_ref in enumerate(net_refs):
        net_all[at] = net_ref[...]
    spread_all[...] = jnp.zeros(spread_all.shape, jnp.float32)

    def spot(line, branch):
        block = pattern_smem[line, branch]
        owner = block // per_dev
        column = pl.multiple_of(lax.rem(block, per_dev) * BLK, BLK)
        step = lax.bitwise_xor(my_pair, owner // 2)
        side = jnp.where(lax.rem(owner, 2) == my_side, 0, half)
        return side + step, column

    spots = [[spot(line, branch) for branch in range(branches)] for line in range(line_blocks)]
    tables = [blocks_ref.at[line] for line in range(line_blocks)]
    changes = []
    for line in range(line_blocks):
        picked = [net_all[at, :, pl.ds(column, BLK)] for at, column in spots[line]]
        flow = jnp.dot(
            jnp.concatenate(picked, axis=1),
            tables[line][...].reshape(branches * BLK, BLK),
            preferred_element_type=jnp.float32,
        )
        lanes = pl.ds(line * BLK, BLK)
        limit = limits_ref[lanes].reshape(1, BLK)
        upper_old = jnp.concatenate([old_ref[0, hour, :, lanes] for hour in range(hours)], axis=0)
        lower_old = jnp.concatenate([old_ref[1, hour, :, lanes] for hour in range(hours)], axis=0)
        upper = jnp.maximum(0.0, upper_old + (flow - limit))
        lower = jnp.maximum(0.0, lower_old + (-flow - limit))
        for hour in range(hours):
            here = slice(hour * scn_dev, (hour + 1) * scn_dev)
            new_ref[0, hour, :, lanes] = upper[here]
            new_ref[1, hour, :, lanes] = lower[here]
        changes.append(((upper - upper_old) - (lower - lower_old)).astype(jnp.bfloat16))
    new_copy.start()
    for line in range(line_blocks):
        spread = lax.dot_general(
            changes[line],
            tables[line][...].reshape(branches * BLK, BLK),
            (((1,), (1,)), ((), ())),
            preferred_element_type=jnp.float32,
        )
        held = [spread_all[at, :, pl.ds(column, BLK)] for at, column in spots[line]]
        for branch, (at, column) in enumerate(spots[line]):
            spread_all[at, :, pl.ds(column, BLK)] = (
                held[branch] + spread[:, branch * BLK : (branch + 1) * BLK]
            )
    far_out[:half] = spread_all[half:].astype(jnp.bfloat16)
    far_out[half] = spread_all[DIRECT].astype(jnp.bfloat16)
    price_copy.wait()
    part = lax.axis_index("gen")
    for hour in range(hours):
        price = price_ref[hour, :scn_dev, :]
        for other in range(1, price_ref.shape[1] // scn_dev):
            price = jnp.where(part == other, price_ref[hour, other * scn_dev : (other + 1) * scn_dev, :], price)
        here = slice(hour * scn_dev, (hour + 1) * scn_dev)
        spread_all[0, here, :] = spread_all[0, here, :] - price
    new_copy.wait()


def run_lines(pattern, nets, blocks, limits, old, bus_price):
    ring = len(nets)
    half = ring // 2
    smem = pl.BlockSpec(memory_space=pltpu.SMEM)
    vmem = pl.BlockSpec(memory_space=pltpu.VMEM)
    hbm = pl.BlockSpec(memory_space=pltpu.HBM)
    return pl.pallas_call(
        functools.partial(line_kernel, half=half),
        out_shape=(
            jax.ShapeDtypeStruct(old.shape, jnp.float32),
            jax.ShapeDtypeStruct((ring,) + nets[0].shape, jnp.float32),
            jax.ShapeDtypeStruct((half + 1,) + nets[0].shape, jnp.bfloat16),
        ),
        in_specs=[smem] + [vmem] * (ring + 3) + [hbm],
        out_specs=(hbm, vmem, vmem),
        scratch_shapes=[
            pltpu.VMEM((ring,) + nets[0].shape, jnp.bfloat16),
            pltpu.VMEM(old.shape, jnp.float32),
            pltpu.VMEM(bus_price.shape, jnp.float32),
            pltpu.SemaphoreType.DMA((2,)),
        ],
        compiler_params=pltpu.CompilerParams(vmem_limit_bytes=24 * 2**20),
        name="lines",
    )(
        pattern,
        *nets,
        blocks,
        limits,
        old,
        pltpu.with_memory_space_constraint(bus_price, pltpu.HBM),
    )


def price_kernel(*refs):
    share_refs, (out_ref, share_all) = refs[:-2], refs[-2:]
    hours = out_ref.shape[0]
    parts = len(share_refs)
    scn_dev = out_ref.shape[1] // parts
    me = lax.axis_index("gen")
    for step, share in enumerate(share_refs):
        share_all[step] = share[...]
    steps = [lax.bitwise_xor(me, part) for part in range(parts)]
    for hour in range(hours):
        less = [share_all[step, hour * scn_dev : (hour + 1) * scn_dev, :] for step in steps]
        out_ref[hour] = -jnp.concatenate(less, axis=0)


def shards(
    bus_price,
    bus_demand,
    multipliers,
    line_limits,
    ptdf_blocks,
    ptdf_pattern,
    gen_bus,
    state_counts,
    transitions,
    state_level,
    state_cost,
):
    scn_dev, hours, bus_dev = bus_demand.shape
    parts = lax.axis_size("gen")
    ring = lax.axis_size("bus")
    half = ring // 2
    gens = state_level.shape[0]
    row_total = scn_dev * hours
    vmem = pl.BlockSpec(memory_space=pltpu.VMEM)
    roomy = pltpu.CompilerParams(vmem_limit_bytes=24 * 2**20)

    def trade(size, step):
        return [(i, i ^ step) for i in range(size)]

    bus_price = jnp.transpose(bus_price, (1, 0, 2))
    bus_demand = jnp.transpose(bus_demand, (1, 0, 2))
    multipliers = jnp.transpose(multipliers, (0, 2, 1, 3))
    transitions = jnp.transpose(transitions, (1, 0, 2))
    ahead = (bus_demand, ptdf_blocks, multipliers, line_limits, ptdf_pattern)
    plan, *ahead = run_plan(
        state_counts, gen_bus, transitions, state_level, state_cost, bus_price, ahead, parts
    )
    bus_demand, ptdf_blocks, multipliers, line_limits, ptdf_pattern = ahead
    received = lax.all_to_all(plan, "gen", split_axis=0, concat_axis=0, tiled=True)
    net = pl.pallas_call(
        functools.partial(net_kernel, gens=gens),
        out_shape=jax.ShapeDtypeStruct((row_total, bus_dev), jnp.bfloat16),
        in_specs=[vmem, vmem],
        out_specs=vmem,
        compiler_params=roomy,
        name="net",
    )(received, bus_demand)

    far = [lax.ppermute(net, "bus", trade(ring, 2 * step)) for step in range(1, half)]
    handed = [net] + far
    other = [
        lax.ppermute(net, "bus", trade(ring, 2 * step + 1))
        if step == DIRECT
        else lax.ppermute(handed[step], "bus", trade(ring, 1))
        for step in range(half)
    ]
    new_multipliers, spread, far_part = run_lines(
        ptdf_pattern, [net] + far + other, ptdf_blocks, line_limits, multipliers, bus_price
    )

    own_change = spread[0]
    for step in range(half):
        if step == DIRECT:
            shares = [
                lax.ppermute(far_part[half], "bus", trade(ring, 2 * step)),
                lax.ppermute(far_part[step], "bus", trade(ring, 2 * step + 1)),
            ]
        else:
            shares = [lax.ppermute(far_part[step], "bus", trade(ring, 1))]
            if step:
                share = (spread[step] + shares[0].astype(jnp.float32)).astype(jnp.bfloat16)
                shares = [lax.ppermute(share, "bus", trade(ring, 2 * step))]
        for share in shares:
            own_change = own_change + share.astype(jnp.float32)
    shares = [own_change]
    for step in range(1, parts):
        moved, by = (shares[step - 1], 1) if step % 2 else (own_change, step)
        shares.append(lax.ppermute(moved, "gen", trade(parts, by)))
    new_price = pl.pallas_call(
        price_kernel,
        out_shape=jax.ShapeDtypeStruct(bus_price.shape, jnp.float32),
        in_specs=[vmem] * parts,
        out_specs=vmem,
        scratch_shapes=[pltpu.VMEM((parts, row_total, bus_dev), jnp.float32)],
        compiler_params=roomy,
        name="price",
    )(*shares)
    return (jnp.transpose(new_multipliers, (0, 2, 1, 3)), jnp.transpose(new_price, (1, 0, 2)))


def solution(mesh):
    in_specs = (
        P(None, None, "bus"),
        P("gen", None, "bus"),
        P(None, "gen", None, "bus"),
        P("bus"),
        P("bus", None, None, None),
        P("bus", None),
        P(("gen", "bus")),
        P(("gen", "bus")),
        P(("gen", "bus"), None, None),
        P(("gen", "bus"), None),
        P(("gen", "bus"), None),
    )
    out_specs = (P(None, "gen", None, "bus"), P(None, None, "bus"))
    return jax.shard_map(shards, mesh=mesh, in_specs=in_specs, out_specs=out_specs, check_vma=False)
```

```python
import functools

import jax
import jax.numpy as jnp
from jax import lax
from jax.experimental import pallas as pl
from jax.experimental.pallas import tpu as pltpu
from jax.sharding import PartitionSpec as P

STATES = 512
HALF = 256
BLK = 128
NNZB = 16
GROUP = 16
BIG_GROUP = 6
LANES = 128
AHEAD = 5
DIRECT = 1
SUBLANES = 8


def exact_pieces(values):
    high = values.astype(jnp.bfloat16)
    rest = values - high.astype(jnp.float32)
    middle = rest.astype(jnp.bfloat16)
    low = (rest - middle.astype(jnp.float32)).astype(jnp.bfloat16)
    return jnp.concatenate([high, middle, low], axis=0)


def add_pieces(product):
    count = product.shape[0] // 3
    return product[:count] + (product[count : 2 * count] + product[2 * count :])


def plan_kernel(*refs, gens, parts):
    (counts_hbm, bus_hbm, trans_hbm, level_hbm, cost_hbm, price_hbm), refs = refs[:6], refs[6:]
    ahead_hbm, refs = refs[:AHEAD], refs[AHEAD:]
    out_ref, refs = refs[0], refs[1:]
    ahead_refs, refs = refs[:AHEAD], refs[AHEAD:]
    (
        counts_smem,
        bus_smem,
        trans_ref,
        level_ref,
        cost_ref,
        price_ref,
        order,
        level_slot,
        cost_slot,
        gen_price,
        big_table,
        small_table,
        big_state,
        small_state,
        sems,
    ) = refs
    sources = (counts_hbm, bus_hbm, trans_hbm, level_hbm, cost_hbm, price_hbm) + ahead_hbm
    targets = (counts_smem, bus_smem, trans_ref, level_ref, cost_ref, price_ref) + ahead_refs
    copies = [
        pltpu.make_async_copy(source, target, sems.at[at])
        for at, (source, target) in enumerate(zip(sources, targets))
    ]
    for copy in copies:
        copy.start()
    hours, scn, bus_dev = price_ref.shape
    big_total = BIG_GROUP * (gens // GROUP)
    scn_dev = scn // parts
    per_row = LANES // gens
    for copy in copies[:2]:
        copy.wait()

    def place(gen, taken):
        big = (counts_smem[gen] > HALF).astype(jnp.int32)
        slot = jnp.where(big == 1, taken, gens - 1 - (gen - taken))
        order[slot] = gen
        return taken + big

    lax.fori_loop(0, gens, place, jnp.int32(0))

    for copy in copies[2:6]:
        copy.wait()
    lane = lax.broadcasted_iota(jnp.int32, (1, LANES), 1)
    local_row = jnp.zeros((1, LANES), jnp.int32)
    bus_row = jnp.zeros((1, LANES), jnp.int32)
    for slot in range(gens):
        local = lax.rem(bus_smem[order[slot]], bus_dev)
        local_row = jnp.where(lane == slot, local, local_row)
        bus_row = jnp.where(lane == slot, local, bus_row)
    chooser = (
        lax.broadcasted_iota(jnp.int32, (bus_dev, LANES), 0) == local_row
    ).astype(jnp.bfloat16)
    picked = jnp.dot(
        exact_pieces(price_ref[...].reshape(hours * scn, bus_dev)),
        chooser,
        preferred_element_type=jnp.float32,
    )
    gen_price[...] = add_pieces(picked).reshape(hours, scn, LANES)

    state_ids = lax.broadcasted_iota(jnp.int32, (1, STATES), 1)
    spans = []
    for slot in range(gens):
        gen = order[slot]
        span = STATES if slot < big_total else HALF
        spans.append(span)
        level_slot[slot] = jnp.broadcast_to(level_ref[pl.ds(gen, 1), :], (SUBLANES, STATES))
        cost_row = jnp.where(state_ids < counts_smem[gen], cost_ref[pl.ds(gen, 1), :], 1e30)
        cost_slot[slot] = jnp.broadcast_to(cost_row, (SUBLANES, STATES))
        successors = [trans_ref[branch, pl.ds(gen, 1), :] for branch in range(trans_ref.shape[0])]
        table = big_table.at[slot] if slot < big_total else small_table.at[slot - big_total]
        for first in range(0, span, HALF):
            rows = lax.broadcasted_iota(jnp.int32, (HALF, span), 0).astype(jnp.float32).astype(jnp.bfloat16)
            one = jnp.ones((HALF, span), jnp.bfloat16)
            none = jnp.zeros((HALF, span), jnp.bfloat16)
            total = none
            for row in successors:
                shifted = (row[:, :span] - first).astype(jnp.float32).astype(jnp.bfloat16)
                total = total + jnp.where(rows == shifted, one, none)
            table[pl.ds(first, HALF), :] = total

    def repeat_rows(block, copies):
        return block if copies == 1 else jnp.concatenate([block] * copies, axis=0)

    shares = [None] * gens
    outs = [jnp.zeros((scn, LANES), jnp.float32) for _ in range(-(-hours // per_row))]
    for hour in range(hours - 1, -1, -1):
        chains = hours - 1 - hour
        for slot in range(gens):
            span = spans[slot]
            if slot < big_total:
                state, table = big_state.at[slot], big_table.at[slot]
            else:
                state, table = small_state.at[slot - big_total], small_table.at[slot - big_total]
            level = repeat_rows(level_slot[slot][:, :span], scn // SUBLANES)
            cost = repeat_rows(cost_slot[slot][:, :span], scn // SUBLANES)
            price = gen_price[hour][:, slot : slot + 1]
            weight = jnp.exp(price * level - cost)
            if chains > 0:
                weight = weight * shares[slot]
            base = weight if chains == 0 else weight * state[:scn, :]
            total = jnp.sum(base, axis=-1, keepdims=True)
            if hour > 0:
                shares[slot] = 1.0 / total
                pieces = [base.astype(jnp.bfloat16)]
                for chain in range(chains):
                    pieces.append(
                        (weight * state[(chain + 1) * scn : (chain + 2) * scn, :]).astype(jnp.bfloat16)
                    )
                pieces.append((base * level).astype(jnp.bfloat16))
                moved = jnp.dot(
                    jnp.concatenate(pieces, axis=0), table[...], preferred_element_type=jnp.float32
                )
                state[: (chains + 2) * scn, :] = moved
            else:
                for at in range(hours):
                    if at == 0:
                        marked = base * level
                    else:
                        chain = hours - 1 - at
                        marked = weight * state[(chain + 1) * scn : (chain + 2) * scn, :]
                    mean = jnp.sum(marked, axis=-1, keepdims=True) / total
                    here = lane == (at % per_row) * gens + slot
                    outs[at // per_row] = jnp.where(here, mean, outs[at // per_row])
    for slot in range(gens):
        here = lane == (hours % per_row) * gens + slot
        bus = jnp.sum(jnp.where(lane == slot, bus_row, 0)).astype(jnp.float32)
        outs[-1] = jnp.where(here, bus, outs[-1])
    for part in range(parts):
        for row, block in enumerate(outs):
            out_ref[part, row] = block[part * scn_dev : (part + 1) * scn_dev, :]
    for copy in copies[6:]:
        copy.wait()


def run_plan(counts, gen_bus, transitions, level, cost, bus_price, ahead, parts):
    hours, scn, _ = bus_price.shape
    gens = level.shape[0]
    big_total = BIG_GROUP * (gens // GROUP)
    rows = -(-hours // (LANES // gens))
    hbm = pl.BlockSpec(memory_space=pltpu.HBM)
    vmem = pl.BlockSpec(memory_space=pltpu.VMEM)
    return pl.pallas_call(
        functools.partial(plan_kernel, gens=gens, parts=parts),
        out_shape=(pltpu.VMEM((parts, rows, scn // parts, LANES), jnp.float32),)
        + tuple(pltpu.VMEM(array.shape, array.dtype) for array in ahead),
        in_specs=[hbm] * (6 + len(ahead)),
        out_specs=(vmem,) * (1 + len(ahead)),
        scratch_shapes=[
            pltpu.SMEM(counts.shape, jnp.int32),
            pltpu.SMEM(gen_bus.shape, jnp.int32),
            pltpu.VMEM(transitions.shape, jnp.int32),
            pltpu.VMEM(level.shape, jnp.float32),
            pltpu.VMEM(cost.shape, jnp.float32),
            pltpu.VMEM(bus_price.shape, jnp.float32),
            pltpu.SMEM((gens,), jnp.int32),
            pltpu.VMEM((gens, SUBLANES, STATES), jnp.float32),
            pltpu.VMEM((gens, SUBLANES, STATES), jnp.float32),
            pltpu.VMEM((hours, scn, LANES), jnp.float32),
            pltpu.VMEM((big_total, STATES, STATES), jnp.bfloat16),
            pltpu.VMEM((gens - big_total, HALF, HALF), jnp.bfloat16),
            pltpu.VMEM((big_total, (hours + 1) * scn, STATES), jnp.float32),
            pltpu.VMEM((gens - big_total, (hours + 1) * scn, HALF), jnp.float32),
            pltpu.SemaphoreType.DMA((6 + len(ahead),)),
        ],
        compiler_params=pltpu.CompilerParams(vmem_limit_bytes=32 * 2**20),
        name="plan",
    )(
        *(
            pltpu.with_memory_space_constraint(array, pltpu.HBM)
            for array in (counts, gen_bus, transitions, level, cost, bus_price) + ahead
        )
    )


def net_kernel(plan_ref, demand_ref, net_ref, *, gens):
    parts, rows, scn_dev, _ = plan_ref.shape
    hours, _, bus_dev = demand_ref.shape
    per_row = LANES // gens
    lane = lax.broadcasted_iota(jnp.int32, (1, LANES), 1)
    bus_ids = lax.broadcasted_iota(jnp.int32, (bus_dev, LANES), 0).astype(jnp.float32)

    def of_hour(hour):
        start = (hour % per_row) * gens
        return (lane >= start) & (lane < start + gens)

    left, places = [], []
    for part in range(parts):
        values = [plan_ref[part, row] for row in range(rows)]
        left.append(
            jnp.concatenate(
                [jnp.where(of_hour(hour), values[hour // per_row], 0.0) for hour in range(hours)], axis=0
            )
        )
        bus = jnp.where(of_hour(hours), values[-1][:1, :], 0.0)
        bus = jnp.broadcast_to(bus, (SUBLANES, LANES))
        shift = gens
        while shift < LANES:
            bus = bus + pltpu.roll(bus, shift, 1)
            shift *= 2
        places.append((bus_ids == bus[:1, :]).astype(jnp.bfloat16))
    left = jnp.concatenate(left, axis=1)
    placed = lax.dot_general(
        exact_pieces(left),
        jnp.concatenate(places, axis=1),
        (((1,), (1,)), ((), ())),
        preferred_element_type=jnp.float32,
    )
    injections = add_pieces(placed)
    demand = jnp.concatenate([demand_ref[hour] for hour in range(hours)], axis=0)
    net_ref[...] = (injections - demand).astype(jnp.bfloat16)


def line_kernel(pattern_smem, *refs, half):
    net_refs, refs = refs[: 2 * half], refs[2 * half :]
    blocks_ref, limits_ref, old_ref, price_hbm, new_hbm, spread_all, far_out = refs[:7]
    net_all, new_ref, price_ref, sems = refs[7:]
    price_copy = pltpu.make_async_copy(price_hbm, price_ref, sems.at[0])
    price_copy.start()
    new_copy = pltpu.make_async_copy(new_ref, new_hbm, sems.at[1])
    line_blocks, branches = pattern_smem.shape
    _, hours, scn_dev, _ = old_ref.shape
    bus_dev = net_refs[0].shape[1]
    per_dev = bus_dev // BLK
    me = lax.axis_index("bus")
    my_pair, my_side = me // 2, lax.rem(me, 2)

    for at, net_ref in enumerate(net_refs):
        net_all[at] = net_ref[...]
    spread_all[...] = jnp.zeros(spread_all.shape, jnp.float32)

    def spot(line, branch):
        block = pattern_smem[line, branch]
        owner = block // per_dev
        column = pl.multiple_of(lax.rem(block, per_dev) * BLK, BLK)
        step = lax.bitwise_xor(my_pair, owner // 2)
        side = jnp.where(lax.rem(owner, 2) == my_side, 0, half)
        return side + step, column

    spots = [[spot(line, branch) for branch in range(branches)] for line in range(line_blocks)]
    tables = [blocks_ref.at[line] for line in range(line_blocks)]
    changes = []
    for line in range(line_blocks):
        picked = [net_all[at, :, pl.ds(column, BLK)] for at, column in spots[line]]
        flow = jnp.dot(
            jnp.concatenate(picked, axis=1),
            tables[line][...].reshape(branches * BLK, BLK),
            preferred_element_type=jnp.float32,
        )
        lanes = pl.ds(line * BLK, BLK)
        limit = limits_ref[lanes].reshape(1, BLK)
        upper_old = jnp.concatenate([old_ref[0, hour, :, lanes] for hour in range(hours)], axis=0)
        lower_old = jnp.concatenate([old_ref[1, hour, :, lanes] for hour in range(hours)], axis=0)
        upper = jnp.maximum(0.0, upper_old + (flow - limit))
        lower = jnp.maximum(0.0, lower_old + (-flow - limit))
        for hour in range(hours):
            here = slice(hour * scn_dev, (hour + 1) * scn_dev)
            new_ref[0, hour, :, lanes] = upper[here]
            new_ref[1, hour, :, lanes] = lower[here]
        changes.append(((upper - upper_old) - (lower - lower_old)).astype(jnp.bfloat16))
    new_copy.start()
    for line in range(line_blocks):
        spread = lax.dot_general(
            changes[line],
            tables[line][...].reshape(branches * BLK, BLK),
            (((1,), (1,)), ((), ())),
            preferred_element_type=jnp.float32,
        )
        held = [spread_all[at, :, pl.ds(column, BLK)] for at, column in spots[line]]
        for branch, (at, column) in enumerate(spots[line]):
            spread_all[at, :, pl.ds(column, BLK)] = (
                held[branch] + spread[:, branch * BLK : (branch + 1) * BLK]
            )
    far_out[:half] = spread_all[half:].astype(jnp.bfloat16)
    far_out[half] = spread_all[DIRECT].astype(jnp.bfloat16)
    price_copy.wait()
    part = lax.axis_index("gen")
    for hour in range(hours):
        price = price_ref[hour, :scn_dev, :]
        for other in range(1, price_ref.shape[1] // scn_dev):
            price = jnp.where(part == other, price_ref[hour, other * scn_dev : (other + 1) * scn_dev, :], price)
        here = slice(hour * scn_dev, (hour + 1) * scn_dev)
        spread_all[0, here, :] = spread_all[0, here, :] - price
    new_copy.wait()


def run_lines(pattern, nets, blocks, limits, old, bus_price):
    ring = len(nets)
    half = ring // 2
    smem = pl.BlockSpec(memory_space=pltpu.SMEM)
    vmem = pl.BlockSpec(memory_space=pltpu.VMEM)
    hbm = pl.BlockSpec(memory_space=pltpu.HBM)
    return pl.pallas_call(
        functools.partial(line_kernel, half=half),
        out_shape=(
            jax.ShapeDtypeStruct(old.shape, jnp.float32),
            jax.ShapeDtypeStruct((ring,) + nets[0].shape, jnp.float32),
            jax.ShapeDtypeStruct((half + 1,) + nets[0].shape, jnp.bfloat16),
        ),
        in_specs=[smem] + [vmem] * (ring + 3) + [hbm],
        out_specs=(hbm, vmem, vmem),
        scratch_shapes=[
            pltpu.VMEM((ring,) + nets[0].shape, jnp.bfloat16),
            pltpu.VMEM(old.shape, jnp.float32),
            pltpu.VMEM(bus_price.shape, jnp.float32),
            pltpu.SemaphoreType.DMA((2,)),
        ],
        compiler_params=pltpu.CompilerParams(vmem_limit_bytes=24 * 2**20),
        name="lines",
    )(
        pattern,
        *nets,
        blocks,
        limits,
        old,
        pltpu.with_memory_space_constraint(bus_price, pltpu.HBM),
    )


def price_kernel(*refs):
    share_refs, (out_ref, share_all) = refs[:-2], refs[-2:]
    hours = out_ref.shape[0]
    parts = len(share_refs)
    scn_dev = out_ref.shape[1] // parts
    me = lax.axis_index("gen")
    for step, share in enumerate(share_refs):
        share_all[step] = share[...]
    steps = [lax.bitwise_xor(me, part) for part in range(parts)]
    for hour in range(hours):
        less = [share_all[step, hour * scn_dev : (hour + 1) * scn_dev, :] for step in steps]
        out_ref[hour] = -jnp.concatenate(less, axis=0)


def shards(
    bus_price,
    bus_demand,
    multipliers,
    line_limits,
    ptdf_blocks,
    ptdf_pattern,
    gen_bus,
    state_counts,
    transitions,
    state_level,
    state_cost,
):
    scn_dev, hours, bus_dev = bus_demand.shape
    parts = lax.axis_size("gen")
    ring = lax.axis_size("bus")
    half = ring // 2
    gens = state_level.shape[0]
    row_total = scn_dev * hours
    vmem = pl.BlockSpec(memory_space=pltpu.VMEM)
    roomy = pltpu.CompilerParams(vmem_limit_bytes=24 * 2**20)

    def trade(size, step):
        return [(i, i ^ step) for i in range(size)]

    bus_price = jnp.transpose(bus_price, (1, 0, 2))
    bus_demand = jnp.transpose(bus_demand, (1, 0, 2))
    multipliers = jnp.transpose(multipliers, (0, 2, 1, 3))
    transitions = jnp.transpose(transitions, (1, 0, 2))
    ahead = (bus_demand, ptdf_blocks, multipliers, line_limits, ptdf_pattern)
    plan, *ahead = run_plan(
        state_counts, gen_bus, transitions, state_level, state_cost, bus_price, ahead, parts
    )
    bus_demand, ptdf_blocks, multipliers, line_limits, ptdf_pattern = ahead
    received = lax.all_to_all(plan, "gen", split_axis=0, concat_axis=0, tiled=True)
    net = pl.pallas_call(
        functools.partial(net_kernel, gens=gens),
        out_shape=jax.ShapeDtypeStruct((row_total, bus_dev), jnp.bfloat16),
        in_specs=[vmem, vmem],
        out_specs=vmem,
        compiler_params=roomy,
        name="net",
    )(received, bus_demand)

    far = [lax.ppermute(net, "bus", trade(ring, 2 * step)) for step in range(1, half)]
    handed = [net] + far
    other = [
        lax.ppermute(net, "bus", trade(ring, 2 * step + 1))
        if step == DIRECT
        else lax.ppermute(handed[step], "bus", trade(ring, 1))
        for step in range(half)
    ]
    new_multipliers, spread, far_part = run_lines(
        ptdf_pattern, [net] + far + other, ptdf_blocks, line_limits, multipliers, bus_price
    )

    own_change = spread[0]
    for step in range(half):
        if step == DIRECT:
            shares = [
                lax.ppermute(far_part[half], "bus", trade(ring, 2 * step)),
                lax.ppermute(far_part[step], "bus", trade(ring, 2 * step + 1)),
            ]
        else:
            shares = [lax.ppermute(far_part[step], "bus", trade(ring, 1))]
            if step:
                share = (spread[step] + shares[0].astype(jnp.float32)).astype(jnp.bfloat16)
                shares = [lax.ppermute(share, "bus", trade(ring, 2 * step))]
        for share in shares:
            own_change = own_change + share.astype(jnp.float32)
    shares = [own_change]
    for step in range(1, parts):
        moved, by = (shares[step - 1], 1) if step % 2 else (own_change, step)
        shares.append(lax.ppermute(moved, "gen", trade(parts, by)))
    new_price = pl.pallas_call(
        price_kernel,
        out_shape=jax.ShapeDtypeStruct(bus_price.shape, jnp.float32),
        in_specs=[vmem] * parts,
        out_specs=vmem,
        scratch_shapes=[pltpu.VMEM((parts, row_total, bus_dev), jnp.float32)],
        compiler_params=roomy,
        name="price",
    )(*shares)
    return (jnp.transpose(new_multipliers, (0, 2, 1, 3)), jnp.transpose(new_price, (1, 0, 2)))


def solution(mesh):
    in_specs = (
        P(None, None, "bus"),
        P("gen", None, "bus"),
        P(None, "gen", None, "bus"),
        P("bus"),
        P("bus", None, None, None),
        P("bus", None),
        P(("gen", "bus")),
        P(("gen", "bus")),
        P(("gen", "bus"), None, None),
        P(("gen", "bus"), None),
        P(("gen", "bus"), None),
    )
    out_specs = (P(None, "gen", None, "bus"), P(None, None, "bus"))
    return jax.shard_map(shards, mesh=mesh, in_specs=in_specs, out_specs=out_specs, check_vma=False)
```

```python
import functools

import jax
import jax.numpy as jnp
from jax import lax
from jax.experimental import pallas as pl
from jax.experimental.pallas import tpu as pltpu
from jax.sharding import PartitionSpec as P

STATES = 512
HALF = 256
BLK = 128
NNZB = 16
GROUP = 16
BIG_GROUP = 6
LANES = 128
AHEAD = 5
DIRECT = 1
SUBLANES = 8


def exact_pieces(values):
    high = values.astype(jnp.bfloat16)
    rest = values - high.astype(jnp.float32)
    middle = rest.astype(jnp.bfloat16)
    low = (rest - middle.astype(jnp.float32)).astype(jnp.bfloat16)
    return jnp.concatenate([high, middle, low], axis=0)


def add_pieces(product):
    count = product.shape[0] // 3
    return product[:count] + (product[count : 2 * count] + product[2 * count :])


def plan_kernel(*refs, gens, parts):
    (counts_hbm, bus_hbm, trans_hbm, level_hbm, cost_hbm, price_hbm), refs = refs[:6], refs[6:]
    ahead_hbm, refs = refs[:AHEAD], refs[AHEAD:]
    out_ref, refs = refs[0], refs[1:]
    ahead_refs, refs = refs[:AHEAD], refs[AHEAD:]
    (
        counts_smem,
        bus_smem,
        trans_ref,
        level_ref,
        cost_ref,
        price_ref,
        order,
        level_slot,
        cost_slot,
        gen_price,
        big_table,
        small_table,
        big_state,
        small_state,
        sems,
    ) = refs
    sources = (counts_hbm, bus_hbm, trans_hbm, level_hbm, cost_hbm, price_hbm) + ahead_hbm
    targets = (counts_smem, bus_smem, trans_ref, level_ref, cost_ref, price_ref) + ahead_refs
    copies = [
        pltpu.make_async_copy(source, target, sems.at[at])
        for at, (source, target) in enumerate(zip(sources, targets))
    ]
    for copy in copies:
        copy.start()
    hours, scn, bus_dev = price_ref.shape
    big_total = BIG_GROUP * (gens // GROUP)
    scn_dev = scn // parts
    per_row = LANES // gens
    for copy in copies[:2]:
        copy.wait()

    def place(gen, taken):
        big = (counts_smem[gen] > HALF).astype(jnp.int32)
        slot = jnp.where(big == 1, taken, gens - 1 - (gen - taken))
        order[slot] = gen
        return taken + big

    lax.fori_loop(0, gens, place, jnp.int32(0))

    for copy in copies[2:6]:
        copy.wait()
    lane = lax.broadcasted_iota(jnp.int32, (1, LANES), 1)
    local_row = jnp.zeros((1, LANES), jnp.int32)
    bus_row = jnp.zeros((1, LANES), jnp.int32)
    for slot in range(gens):
        local = lax.rem(bus_smem[order[slot]], bus_dev)
        local_row = jnp.where(lane == slot, local, local_row)
        bus_row = jnp.where(lane == slot, local, bus_row)
    chooser = (
        lax.broadcasted_iota(jnp.int32, (bus_dev, LANES), 0) == local_row
    ).astype(jnp.bfloat16)
    picked = jnp.dot(
        exact_pieces(price_ref[...].reshape(hours * scn, bus_dev)),
        chooser,
        preferred_element_type=jnp.float32,
    )
    gen_price[...] = add_pieces(picked).reshape(hours, scn, LANES)

    state_ids = lax.broadcasted_iota(jnp.int32, (1, STATES), 1)
    spans = []
    for slot in range(gens):
        gen = order[slot]
        span = STATES if slot < big_total else HALF
        spans.append(span)
        level_slot[slot] = jnp.broadcast_to(level_ref[pl.ds(gen, 1), :], (SUBLANES, STATES))
        cost_row = jnp.where(state_ids < counts_smem[gen], cost_ref[pl.ds(gen, 1), :], 1e30)
        cost_slot[slot] = jnp.broadcast_to(cost_row, (SUBLANES, STATES))
        successors = [trans_ref[branch, pl.ds(gen, 1), :] for branch in range(trans_ref.shape[0])]
        table = big_table.at[slot] if slot < big_total else small_table.at[slot - big_total]
        for first in range(0, span, HALF):
            rows = lax.broadcasted_iota(jnp.int32, (HALF, span), 0).astype(jnp.float32).astype(jnp.bfloat16)
            one = jnp.ones((HALF, span), jnp.bfloat16)
            none = jnp.zeros((HALF, span), jnp.bfloat16)
            total = none
            for row in successors:
                shifted = (row[:, :span] - first).astype(jnp.float32).astype(jnp.bfloat16)
                total = total + jnp.where(rows == shifted, one, none)
            table[pl.ds(first, HALF), :] = total

    def repeat_rows(block, copies):
        return block if copies == 1 else jnp.concatenate([block] * copies, axis=0)

    shares = [None] * gens
    outs = [jnp.zeros((scn, LANES), jnp.float32) for _ in range(-(-hours // per_row))]
    for hour in range(hours - 1, -1, -1):
        chains = hours - 1 - hour
        for slot in range(gens):
            span = spans[slot]
            if slot < big_total:
                state, table = big_state.at[slot], big_table.at[slot]
            else:
                state, table = small_state.at[slot - big_total], small_table.at[slot - big_total]
            level = repeat_rows(level_slot[slot][:, :span], scn // SUBLANES)
            cost = repeat_rows(cost_slot[slot][:, :span], scn // SUBLANES)
            price = gen_price[hour][:, slot : slot + 1]
            weight = jnp.exp(price * level - cost)
            if chains > 0:
                weight = weight * shares[slot]
            base = weight if chains == 0 else weight * state[:scn, :]
            total = jnp.sum(base, axis=-1, keepdims=True)
            if hour > 0:
                shares[slot] = 1.0 / total
                pieces = [base.astype(jnp.bfloat16)]
                for chain in range(chains):
                    pieces.append(
                        (weight * state[(chain + 1) * scn : (chain + 2) * scn, :]).astype(jnp.bfloat16)
                    )
                pieces.append((base * level).astype(jnp.bfloat16))
                moved = jnp.dot(
                    jnp.concatenate(pieces, axis=0), table[...], preferred_element_type=jnp.float32
                )
                state[: (chains + 2) * scn, :] = moved
            else:
                for at in range(hours):
                    if at == 0:
                        marked = base * level
                    else:
                        chain = hours - 1 - at
                        marked = weight * state[(chain + 1) * scn : (chain + 2) * scn, :]
                    mean = jnp.sum(marked, axis=-1, keepdims=True) / total
                    here = lane == (at % per_row) * gens + slot
                    outs[at // per_row] = jnp.where(here, mean, outs[at // per_row])
    me = lax.axis_index("gen")
    for slot in range(gens):
        here = lane == (hours % per_row) * gens + slot
        bus = jnp.sum(jnp.where(lane == slot, bus_row, 0)).astype(jnp.float32)
        outs[-1] = jnp.where(here, bus, outs[-1])
    for part in range(parts):
        for row, block in enumerate(outs):
            out_ref[lax.bitwise_xor(me, part), row] = block[part * scn_dev : (part + 1) * scn_dev, :]
    for copy in copies[6:]:
        copy.wait()


def run_plan(counts, gen_bus, transitions, level, cost, bus_price, ahead, parts):
    hours, scn, _ = bus_price.shape
    gens = level.shape[0]
    big_total = BIG_GROUP * (gens // GROUP)
    rows = -(-hours // (LANES // gens))
    hbm = pl.BlockSpec(memory_space=pltpu.HBM)
    vmem = pl.BlockSpec(memory_space=pltpu.VMEM)
    return pl.pallas_call(
        functools.partial(plan_kernel, gens=gens, parts=parts),
        out_shape=(pltpu.VMEM((parts, rows, scn // parts, LANES), jnp.float32),)
        + tuple(pltpu.VMEM(array.shape, array.dtype) for array in ahead),
        in_specs=[hbm] * (6 + len(ahead)),
        out_specs=(vmem,) * (1 + len(ahead)),
        scratch_shapes=[
            pltpu.SMEM(counts.shape, jnp.int32),
            pltpu.SMEM(gen_bus.shape, jnp.int32),
            pltpu.VMEM(transitions.shape, jnp.int32),
            pltpu.VMEM(level.shape, jnp.float32),
            pltpu.VMEM(cost.shape, jnp.float32),
            pltpu.VMEM(bus_price.shape, jnp.float32),
            pltpu.SMEM((gens,), jnp.int32),
            pltpu.VMEM((gens, SUBLANES, STATES), jnp.float32),
            pltpu.VMEM((gens, SUBLANES, STATES), jnp.float32),
            pltpu.VMEM((hours, scn, LANES), jnp.float32),
            pltpu.VMEM((big_total, STATES, STATES), jnp.bfloat16),
            pltpu.VMEM((gens - big_total, HALF, HALF), jnp.bfloat16),
            pltpu.VMEM((big_total, (hours + 1) * scn, STATES), jnp.float32),
            pltpu.VMEM((gens - big_total, (hours + 1) * scn, HALF), jnp.float32),
            pltpu.SemaphoreType.DMA((6 + len(ahead),)),
        ],
        compiler_params=pltpu.CompilerParams(vmem_limit_bytes=32 * 2**20),
        name="plan",
    )(
        *(
            pltpu.with_memory_space_constraint(array, pltpu.HBM)
            for array in (counts, gen_bus, transitions, level, cost, bus_price) + ahead
        )
    )


def net_kernel(*refs, gens):
    plan_refs, (demand_ref, net_ref) = refs[:-2], refs[-2:]
    rows, scn_dev = plan_refs[0].shape[1:3]
    hours, _, bus_dev = demand_ref.shape
    per_row = LANES // gens
    lane = lax.broadcasted_iota(jnp.int32, (1, LANES), 1)
    bus_ids = lax.broadcasted_iota(jnp.int32, (bus_dev, LANES), 0).astype(jnp.float32)

    def of_hour(hour):
        start = (hour % per_row) * gens
        return (lane >= start) & (lane < start + gens)

    left, places = [], []
    for plan_ref in plan_refs:
        values = [plan_ref[0, row] for row in range(rows)]
        left.append(
            jnp.concatenate(
                [jnp.where(of_hour(hour), values[hour // per_row], 0.0) for hour in range(hours)], axis=0
            )
        )
        bus = jnp.where(of_hour(hours), values[-1][:1, :], 0.0)
        bus = jnp.broadcast_to(bus, (SUBLANES, LANES))
        shift = gens
        while shift < LANES:
            bus = bus + pltpu.roll(bus, shift, 1)
            shift *= 2
        places.append((bus_ids == bus[:1, :]).astype(jnp.bfloat16))
    left = jnp.concatenate(left, axis=1)
    placed = lax.dot_general(
        exact_pieces(left),
        jnp.concatenate(places, axis=1),
        (((1,), (1,)), ((), ())),
        preferred_element_type=jnp.float32,
    )
    injections = add_pieces(placed)
    demand = jnp.concatenate([demand_ref[hour] for hour in range(hours)], axis=0)
    net_ref[...] = (injections - demand).astype(jnp.bfloat16)


def line_kernel(pattern_smem, *refs, half):
    net_refs, refs = refs[: 2 * half], refs[2 * half :]
    blocks_ref, limits_ref, old_ref, price_hbm, new_hbm, spread_all, far_out = refs[:7]
    net_all, new_ref, price_ref, sems = refs[7:]
    price_copy = pltpu.make_async_copy(price_hbm, price_ref, sems.at[0])
    price_copy.start()
    new_copy = pltpu.make_async_copy(new_ref, new_hbm, sems.at[1])
    line_blocks, branches = pattern_smem.shape
    _, hours, scn_dev, _ = old_ref.shape
    bus_dev = net_refs[0].shape[1]
    per_dev = bus_dev // BLK
    me = lax.axis_index("bus")
    my_pair, my_side = me // 2, lax.rem(me, 2)

    for at, net_ref in enumerate(net_refs):
        net_all[at] = net_ref[...]
    spread_all[...] = jnp.zeros(spread_all.shape, jnp.float32)

    def spot(line, branch):
        block = pattern_smem[line, branch]
        owner = block // per_dev
        column = pl.multiple_of(lax.rem(block, per_dev) * BLK, BLK)
        step = lax.bitwise_xor(my_pair, owner // 2)
        side = jnp.where(lax.rem(owner, 2) == my_side, 0, half)
        return side + step, column

    spots = [[spot(line, branch) for branch in range(branches)] for line in range(line_blocks)]
    tables = [blocks_ref.at[line] for line in range(line_blocks)]
    changes = []
    for line in range(line_blocks):
        picked = [net_all[at, :, pl.ds(column, BLK)] for at, column in spots[line]]
        flow = jnp.dot(
            jnp.concatenate(picked, axis=1),
            tables[line][...].reshape(branches * BLK, BLK),
            preferred_element_type=jnp.float32,
        )
        lanes = pl.ds(line * BLK, BLK)
        limit = limits_ref[lanes].reshape(1, BLK)
        upper_old = jnp.concatenate([old_ref[0, hour, :, lanes] for hour in range(hours)], axis=0)
        lower_old = jnp.concatenate([old_ref[1, hour, :, lanes] for hour in range(hours)], axis=0)
        upper = jnp.maximum(0.0, upper_old + (flow - limit))
        lower = jnp.maximum(0.0, lower_old + (-flow - limit))
        for hour in range(hours):
            here = slice(hour * scn_dev, (hour + 1) * scn_dev)
            new_ref[0, hour, :, lanes] = upper[here]
            new_ref[1, hour, :, lanes] = lower[here]
        changes.append(((upper - upper_old) - (lower - lower_old)).astype(jnp.bfloat16))
    new_copy.start()
    for line in range(line_blocks):
        spread = lax.dot_general(
            changes[line],
            tables[line][...].reshape(branches * BLK, BLK),
            (((1,), (1,)), ((), ())),
            preferred_element_type=jnp.float32,
        )
        held = [spread_all[at, :, pl.ds(column, BLK)] for at, column in spots[line]]
        for branch, (at, column) in enumerate(spots[line]):
            spread_all[at, :, pl.ds(column, BLK)] = (
                held[branch] + spread[:, branch * BLK : (branch + 1) * BLK]
            )
    far_out[:half] = spread_all[half:].astype(jnp.bfloat16)
    far_out[half] = spread_all[DIRECT].astype(jnp.bfloat16)
    price_copy.wait()
    part = lax.axis_index("gen")
    for hour in range(hours):
        price = price_ref[hour, :scn_dev, :]
        for other in range(1, price_ref.shape[1] // scn_dev):
            price = jnp.where(part == other, price_ref[hour, other * scn_dev : (other + 1) * scn_dev, :], price)
        here = slice(hour * scn_dev, (hour + 1) * scn_dev)
        spread_all[0, here, :] = spread_all[0, here, :] - price
    new_copy.wait()


def run_lines(pattern, nets, blocks, limits, old, bus_price):
    ring = len(nets)
    half = ring // 2
    smem = pl.BlockSpec(memory_space=pltpu.SMEM)
    vmem = pl.BlockSpec(memory_space=pltpu.VMEM)
    hbm = pl.BlockSpec(memory_space=pltpu.HBM)
    return pl.pallas_call(
        functools.partial(line_kernel, half=half),
        out_shape=(
            jax.ShapeDtypeStruct(old.shape, jnp.float32),
            jax.ShapeDtypeStruct((ring,) + nets[0].shape, jnp.float32),
            jax.ShapeDtypeStruct((half + 1,) + nets[0].shape, jnp.bfloat16),
        ),
        in_specs=[smem] + [vmem] * (ring + 3) + [hbm],
        out_specs=(hbm, vmem, vmem),
        scratch_shapes=[
            pltpu.VMEM((ring,) + nets[0].shape, jnp.bfloat16),
            pltpu.VMEM(old.shape, jnp.float32),
            pltpu.VMEM(bus_price.shape, jnp.float32),
            pltpu.SemaphoreType.DMA((2,)),
        ],
        compiler_params=pltpu.CompilerParams(vmem_limit_bytes=24 * 2**20),
        name="lines",
    )(
        pattern,
        *nets,
        blocks,
        limits,
        old,
        pltpu.with_memory_space_constraint(bus_price, pltpu.HBM),
    )


def price_kernel(*refs):
    share_refs, (out_ref, share_all) = refs[:-2], refs[-2:]
    hours = out_ref.shape[0]
    parts = len(share_refs)
    scn_dev = out_ref.shape[1] // parts
    me = lax.axis_index("gen")
    for step, share in enumerate(share_refs):
        share_all[step] = share[...]
    steps = [lax.bitwise_xor(me, part) for part in range(parts)]
    for hour in range(hours):
        less = [share_all[step, hour * scn_dev : (hour + 1) * scn_dev, :] for step in steps]
        out_ref[hour] = -jnp.concatenate(less, axis=0)


def shards(
    bus_price,
    bus_demand,
    multipliers,
    line_limits,
    ptdf_blocks,
    ptdf_pattern,
    gen_bus,
    state_counts,
    transitions,
    state_level,
    state_cost,
):
    scn_dev, hours, bus_dev = bus_demand.shape
    parts = lax.axis_size("gen")
    ring = lax.axis_size("bus")
    half = ring // 2
    gens = state_level.shape[0]
    row_total = scn_dev * hours
    vmem = pl.BlockSpec(memory_space=pltpu.VMEM)
    roomy = pltpu.CompilerParams(vmem_limit_bytes=24 * 2**20)

    def trade(size, step):
        return [(i, i ^ step) for i in range(size)]

    bus_price = jnp.transpose(bus_price, (1, 0, 2))
    bus_demand = jnp.transpose(bus_demand, (1, 0, 2))
    multipliers = jnp.transpose(multipliers, (0, 2, 1, 3))
    transitions = jnp.transpose(transitions, (1, 0, 2))
    ahead = (bus_demand, ptdf_blocks, multipliers, line_limits, ptdf_pattern)
    plan, *ahead = run_plan(
        state_counts, gen_bus, transitions, state_level, state_cost, bus_price, ahead, parts
    )
    bus_demand, ptdf_blocks, multipliers, line_limits, ptdf_pattern = ahead
    received = [plan, lax.ppermute(plan[1:2], "gen", trade(parts, 1))]
    for step in range(2, parts, 2):
        both = lax.ppermute(plan[step : step + 2], "gen", trade(parts, step))
        received += [both, lax.ppermute(both[1:], "gen", trade(parts, 1))]
    net = pl.pallas_call(
        functools.partial(net_kernel, gens=gens),
        out_shape=jax.ShapeDtypeStruct((row_total, bus_dev), jnp.bfloat16),
        in_specs=[vmem] * (len(received) + 1),
        out_specs=vmem,
        compiler_params=roomy,
        name="net",
    )(*received, bus_demand)

    far = [lax.ppermute(net, "bus", trade(ring, 2 * step)) for step in range(1, half)]
    handed = [net] + far
    other = [
        lax.ppermute(net, "bus", trade(ring, 2 * step + 1))
        if step == DIRECT
        else lax.ppermute(handed[step], "bus", trade(ring, 1))
        for step in range(half)
    ]
    new_multipliers, spread, far_part = run_lines(
        ptdf_pattern, [net] + far + other, ptdf_blocks, line_limits, multipliers, bus_price
    )

    own_change = spread[0]
    for step in range(half):
        if step == DIRECT:
            shares = [
                lax.ppermute(far_part[half], "bus", trade(ring, 2 * step)),
                lax.ppermute(far_part[step], "bus", trade(ring, 2 * step + 1)),
            ]
        else:
            shares = [lax.ppermute(far_part[step], "bus", trade(ring, 1))]
            if step:
                share = (spread[step] + shares[0].astype(jnp.float32)).astype(jnp.bfloat16)
                shares = [lax.ppermute(share, "bus", trade(ring, 2 * step))]
        for share in shares:
            own_change = own_change + share.astype(jnp.float32)
    shares = [own_change]
    for step in range(1, parts):
        moved, by = (shares[step - 1], 1) if step % 2 else (own_change, step)
        shares.append(lax.ppermute(moved, "gen", trade(parts, by)))
    new_price = pl.pallas_call(
        price_kernel,
        out_shape=jax.ShapeDtypeStruct(bus_price.shape, jnp.float32),
        in_specs=[vmem] * parts,
        out_specs=vmem,
        scratch_shapes=[pltpu.VMEM((parts, row_total, bus_dev), jnp.float32)],
        compiler_params=roomy,
        name="price",
    )(*shares)
    return (jnp.transpose(new_multipliers, (0, 2, 1, 3)), jnp.transpose(new_price, (1, 0, 2)))


def solution(mesh):
    in_specs = (
        P(None, None, "bus"),
        P("gen", None, "bus"),
        P(None, "gen", None, "bus"),
        P("bus"),
        P("bus", None, None, None),
        P("bus", None),
        P(("gen", "bus")),
        P(("gen", "bus")),
        P(("gen", "bus"), None, None),
        P(("gen", "bus"), None),
        P(("gen", "bus"), None),
    )
    out_specs = (P(None, "gen", None, "bus"), P(None, None, "bus"))
    return jax.shard_map(shards, mesh=mesh, in_specs=in_specs, out_specs=out_specs, check_vma=False)
```

```python
import functools

import jax
import jax.numpy as jnp
from jax import lax
from jax.experimental import pallas as pl
from jax.experimental.pallas import tpu as pltpu
from jax.sharding import PartitionSpec as P

STATES = 512
HALF = 256
BLK = 128
NNZB = 16
GROUP = 16
BIG_GROUP = 6
LANES = 128
AHEAD = 5
DIRECT = 1
SUBLANES = 8


def exact_pieces(values):
    high = values.astype(jnp.bfloat16)
    rest = values - high.astype(jnp.float32)
    middle = rest.astype(jnp.bfloat16)
    low = (rest - middle.astype(jnp.float32)).astype(jnp.bfloat16)
    return jnp.concatenate([high, middle, low], axis=0)


def add_pieces(product):
    count = product.shape[0] // 3
    return product[:count] + (product[count : 2 * count] + product[2 * count :])


def plan_kernel(*refs, gens, parts):
    (counts_hbm, bus_hbm, trans_hbm, level_hbm, cost_hbm, price_hbm), refs = refs[:6], refs[6:]
    ahead_hbm, refs = refs[:AHEAD], refs[AHEAD:]
    out_ref, refs = refs[0], refs[1:]
    ahead_refs, refs = refs[:AHEAD], refs[AHEAD:]
    (
        counts_smem,
        bus_smem,
        trans_ref,
        level_ref,
        cost_ref,
        price_ref,
        order,
        level_slot,
        cost_slot,
        gen_price,
        big_table,
        small_table,
        big_state,
        small_state,
        sems,
    ) = refs
    sources = (counts_hbm, bus_hbm, trans_hbm, level_hbm, cost_hbm, price_hbm) + ahead_hbm
    targets = (counts_smem, bus_smem, trans_ref, level_ref, cost_ref, price_ref) + ahead_refs
    copies = [
        pltpu.make_async_copy(source, target, sems.at[at])
        for at, (source, target) in enumerate(zip(sources, targets))
    ]
    for copy in copies:
        copy.start()
    hours, scn, bus_dev = price_ref.shape
    big_total = BIG_GROUP * (gens // GROUP)
    scn_dev = scn // parts
    per_row = LANES // gens
    for copy in copies[:2]:
        copy.wait()

    def place(gen, taken):
        big = (counts_smem[gen] > HALF).astype(jnp.int32)
        slot = jnp.where(big == 1, taken, gens - 1 - (gen - taken))
        order[slot] = gen
        return taken + big

    lax.fori_loop(0, gens, place, jnp.int32(0))

    for copy in copies[2:6]:
        copy.wait()
    lane = lax.broadcasted_iota(jnp.int32, (1, LANES), 1)
    local_row = jnp.zeros((1, LANES), jnp.int32)
    bus_row = jnp.zeros((1, LANES), jnp.int32)
    for slot in range(gens):
        local = lax.rem(bus_smem[order[slot]], bus_dev)
        local_row = jnp.where(lane == slot, local, local_row)
        bus_row = jnp.where(lane == slot, local, bus_row)
    chooser = (
        lax.broadcasted_iota(jnp.int32, (bus_dev, LANES), 0) == local_row
    ).astype(jnp.bfloat16)
    picked = jnp.dot(
        exact_pieces(price_ref[...].reshape(hours * scn, bus_dev)),
        chooser,
        preferred_element_type=jnp.float32,
    )
    gen_price[...] = add_pieces(picked).reshape(hours, scn, LANES)

    state_ids = lax.broadcasted_iota(jnp.int32, (1, STATES), 1)
    spans = []
    for slot in range(gens):
        gen = order[slot]
        span = STATES if slot < big_total else HALF
        spans.append(span)
        level_slot[slot] = jnp.broadcast_to(level_ref[pl.ds(gen, 1), :], (SUBLANES, STATES))
        cost_row = jnp.where(state_ids < counts_smem[gen], cost_ref[pl.ds(gen, 1), :], 1e30)
        cost_slot[slot] = jnp.broadcast_to(cost_row, (SUBLANES, STATES))
        successors = [trans_ref[branch, pl.ds(gen, 1), :] for branch in range(trans_ref.shape[0])]
        table = big_table.at[slot] if slot < big_total else small_table.at[slot - big_total]
        for first in range(0, span, HALF):
            rows = lax.broadcasted_iota(jnp.int32, (HALF, span), 0).astype(jnp.float32).astype(jnp.bfloat16)
            one = jnp.ones((HALF, span), jnp.bfloat16)
            none = jnp.zeros((HALF, span), jnp.bfloat16)
            total = none
            for row in successors:
                shifted = (row[:, :span] - first).astype(jnp.float32).astype(jnp.bfloat16)
                total = total + jnp.where(rows == shifted, one, none)
            table[pl.ds(first, HALF), :] = total

    def repeat_rows(block, copies):
        return block if copies == 1 else jnp.concatenate([block] * copies, axis=0)

    shares = [None] * gens
    outs = [jnp.zeros((scn, LANES), jnp.float32) for _ in range(-(-hours // per_row))]
    for hour in range(hours - 1, -1, -1):
        chains = hours - 1 - hour
        for slot in range(gens):
            span = spans[slot]
            if slot < big_total:
                state, table = big_state.at[slot], big_table.at[slot]
            else:
                state, table = small_state.at[slot - big_total], small_table.at[slot - big_total]
            level = repeat_rows(level_slot[slot][:, :span], scn // SUBLANES)
            cost = repeat_rows(cost_slot[slot][:, :span], scn // SUBLANES)
            price = gen_price[hour][:, slot : slot + 1]
            weight = jnp.exp(price * level - cost)
            if chains > 0:
                weight = weight * shares[slot]
            base = weight if chains == 0 else weight * state[:scn, :]
            total = jnp.sum(base, axis=-1, keepdims=True)
            if hour > 0:
                shares[slot] = 1.0 / total
                pieces = [base.astype(jnp.bfloat16)]
                for chain in range(chains):
                    pieces.append(
                        (weight * state[(chain + 1) * scn : (chain + 2) * scn, :]).astype(jnp.bfloat16)
                    )
                pieces.append((base * level).astype(jnp.bfloat16))
                moved = jnp.dot(
                    jnp.concatenate(pieces, axis=0), table[...], preferred_element_type=jnp.float32
                )
                state[: (chains + 2) * scn, :] = moved
            else:
                for at in range(hours):
                    if at == 0:
                        marked = base * level
                    else:
                        chain = hours - 1 - at
                        marked = weight * state[(chain + 1) * scn : (chain + 2) * scn, :]
                    mean = jnp.sum(marked, axis=-1, keepdims=True) / total
                    here = lane == (at % per_row) * gens + slot
                    outs[at // per_row] = jnp.where(here, mean, outs[at // per_row])
    me = lax.axis_index("gen")
    for slot in range(gens):
        here = lane == (hours % per_row) * gens + slot
        bus = jnp.sum(jnp.where(lane == slot, bus_row, 0)).astype(jnp.float32)
        outs[-1] = jnp.where(here, bus, outs[-1])
    for part in range(parts):
        for row, block in enumerate(outs):
            out_ref[lax.bitwise_xor(me, part), row] = block[part * scn_dev : (part + 1) * scn_dev, :]
    for copy in copies[6:]:
        copy.wait()


def run_plan(counts, gen_bus, transitions, level, cost, bus_price, ahead, parts):
    hours, scn, _ = bus_price.shape
    gens = level.shape[0]
    big_total = BIG_GROUP * (gens // GROUP)
    rows = -(-hours // (LANES // gens))
    hbm = pl.BlockSpec(memory_space=pltpu.HBM)
    vmem = pl.BlockSpec(memory_space=pltpu.VMEM)
    return pl.pallas_call(
        functools.partial(plan_kernel, gens=gens, parts=parts),
        out_shape=(pltpu.VMEM((parts, rows, scn // parts, LANES), jnp.float32),)
        + tuple(pltpu.VMEM(array.shape, array.dtype) for array in ahead),
        in_specs=[hbm] * (6 + len(ahead)),
        out_specs=(vmem,) * (1 + len(ahead)),
        scratch_shapes=[
            pltpu.SMEM(counts.shape, jnp.int32),
            pltpu.SMEM(gen_bus.shape, jnp.int32),
            pltpu.VMEM(transitions.shape, jnp.int32),
            pltpu.VMEM(level.shape, jnp.float32),
            pltpu.VMEM(cost.shape, jnp.float32),
            pltpu.VMEM(bus_price.shape, jnp.float32),
            pltpu.SMEM((gens,), jnp.int32),
            pltpu.VMEM((gens, SUBLANES, STATES), jnp.float32),
            pltpu.VMEM((gens, SUBLANES, STATES), jnp.float32),
            pltpu.VMEM((hours, scn, LANES), jnp.float32),
            pltpu.VMEM((big_total, STATES, STATES), jnp.bfloat16),
            pltpu.VMEM((gens - big_total, HALF, HALF), jnp.bfloat16),
            pltpu.VMEM((big_total, (hours + 1) * scn, STATES), jnp.float32),
            pltpu.VMEM((gens - big_total, (hours + 1) * scn, HALF), jnp.float32),
            pltpu.SemaphoreType.DMA((6 + len(ahead),)),
        ],
        compiler_params=pltpu.CompilerParams(vmem_limit_bytes=32 * 2**20),
        name="plan",
    )(
        *(
            pltpu.with_memory_space_constraint(array, pltpu.HBM)
            for array in (counts, gen_bus, transitions, level, cost, bus_price) + ahead
        )
    )


def net_kernel(*refs, gens):
    plan_refs, (demand_ref, net_ref) = refs[:-2], refs[-2:]
    rows, scn_dev = plan_refs[0].shape[1:3]
    hours, _, bus_dev = demand_ref.shape
    per_row = LANES // gens
    lane = lax.broadcasted_iota(jnp.int32, (1, LANES), 1)
    bus_ids = lax.broadcasted_iota(jnp.int32, (bus_dev, LANES), 0).astype(jnp.float32)

    def of_hour(hour):
        start = (hour % per_row) * gens
        return (lane >= start) & (lane < start + gens)

    left, places = [], []
    for plan_ref in plan_refs:
        values = [plan_ref[0, row] for row in range(rows)]
        left.append(
            jnp.concatenate(
                [jnp.where(of_hour(hour), values[hour // per_row], 0.0) for hour in range(hours)], axis=0
            )
        )
        bus = jnp.where(of_hour(hours), values[-1][:1, :], 0.0)
        bus = jnp.broadcast_to(bus, (SUBLANES, LANES))
        shift = gens
        while shift < LANES:
            bus = bus + pltpu.roll(bus, shift, 1)
            shift *= 2
        places.append((bus_ids == bus[:1, :]).astype(jnp.bfloat16))
    left = jnp.concatenate(left, axis=1)
    placed = lax.dot_general(
        exact_pieces(left),
        jnp.concatenate(places, axis=1),
        (((1,), (1,)), ((), ())),
        preferred_element_type=jnp.float32,
    )
    injections = add_pieces(placed)
    demand = jnp.concatenate([demand_ref[hour] for hour in range(hours)], axis=0)
    net_ref[...] = (injections - demand).astype(jnp.bfloat16)


def line_kernel(pattern_ref, *refs, half):
    net_refs, refs = refs[: 2 * half], refs[2 * half :]
    blocks_ref, limits_ref, old_ref, price_hbm, new_hbm, spread_all, far_out = refs[:7]
    pattern_smem, net_all, new_ref, price_ref, sems = refs[7:]
    pattern_copy = pltpu.make_async_copy(pattern_ref, pattern_smem, sems.at[2])
    pattern_copy.start()
    price_copy = pltpu.make_async_copy(price_hbm, price_ref, sems.at[0])
    price_copy.start()
    new_copy = pltpu.make_async_copy(new_ref, new_hbm, sems.at[1])
    line_blocks, branches = pattern_ref.shape
    _, hours, scn_dev, _ = old_ref.shape
    bus_dev = net_refs[0].shape[1]
    per_dev = bus_dev // BLK
    me = lax.axis_index("bus")
    my_pair, my_side = me // 2, lax.rem(me, 2)

    for at, net_ref in enumerate(net_refs):
        net_all[at] = net_ref[...]
    spread_all[...] = jnp.zeros(spread_all.shape, jnp.float32)
    pattern_copy.wait()

    def spot(line, branch):
        block = pattern_smem[line, branch]
        owner = block // per_dev
        column = pl.multiple_of(lax.rem(block, per_dev) * BLK, BLK)
        step = lax.bitwise_xor(my_pair, owner // 2)
        side = jnp.where(lax.rem(owner, 2) == my_side, 0, half)
        return side + step, column

    spots = [[spot(line, branch) for branch in range(branches)] for line in range(line_blocks)]
    tables = [blocks_ref.at[line] for line in range(line_blocks)]
    changes = []
    for line in range(line_blocks):
        picked = [net_all[at, :, pl.ds(column, BLK)] for at, column in spots[line]]
        flow = jnp.dot(
            jnp.concatenate(picked, axis=1),
            tables[line][...].reshape(branches * BLK, BLK),
            preferred_element_type=jnp.float32,
        )
        lanes = pl.ds(line * BLK, BLK)
        limit = limits_ref[lanes].reshape(1, BLK)
        upper_old = jnp.concatenate([old_ref[0, hour, :, lanes] for hour in range(hours)], axis=0)
        lower_old = jnp.concatenate([old_ref[1, hour, :, lanes] for hour in range(hours)], axis=0)
        upper = jnp.maximum(0.0, upper_old + (flow - limit))
        lower = jnp.maximum(0.0, lower_old + (-flow - limit))
        for hour in range(hours):
            here = slice(hour * scn_dev, (hour + 1) * scn_dev)
            new_ref[0, hour, :, lanes] = upper[here]
            new_ref[1, hour, :, lanes] = lower[here]
        changes.append(((upper - upper_old) - (lower - lower_old)).astype(jnp.bfloat16))
    new_copy.start()
    for line in range(line_blocks):
        spread = lax.dot_general(
            changes[line],
            tables[line][...].reshape(branches * BLK, BLK),
            (((1,), (1,)), ((), ())),
            preferred_element_type=jnp.float32,
        )
        held = [spread_all[at, :, pl.ds(column, BLK)] for at, column in spots[line]]
        for branch, (at, column) in enumerate(spots[line]):
            spread_all[at, :, pl.ds(column, BLK)] = (
                held[branch] + spread[:, branch * BLK : (branch + 1) * BLK]
            )
    far_out[:half] = spread_all[half:].astype(jnp.bfloat16)
    far_out[half] = spread_all[DIRECT].astype(jnp.bfloat16)
    price_copy.wait()
    part = lax.axis_index("gen")
    for hour in range(hours):
        price = price_ref[hour, :scn_dev, :]
        for other in range(1, price_ref.shape[1] // scn_dev):
            price = jnp.where(part == other, price_ref[hour, other * scn_dev : (other + 1) * scn_dev, :], price)
        here = slice(hour * scn_dev, (hour + 1) * scn_dev)
        spread_all[0, here, :] = spread_all[0, here, :] - price
    new_copy.wait()


def run_lines(pattern, nets, blocks, limits, old, bus_price):
    ring = len(nets)
    half = ring // 2
    vmem = pl.BlockSpec(memory_space=pltpu.VMEM)
    hbm = pl.BlockSpec(memory_space=pltpu.HBM)
    return pl.pallas_call(
        functools.partial(line_kernel, half=half),
        out_shape=(
            jax.ShapeDtypeStruct(old.shape, jnp.float32),
            jax.ShapeDtypeStruct((ring,) + nets[0].shape, jnp.float32),
            jax.ShapeDtypeStruct((half + 1,) + nets[0].shape, jnp.bfloat16),
        ),
        in_specs=[vmem] * (ring + 4) + [hbm],
        out_specs=(hbm, vmem, vmem),
        scratch_shapes=[
            pltpu.SMEM(pattern.shape, jnp.int32),
            pltpu.VMEM((ring,) + nets[0].shape, jnp.bfloat16),
            pltpu.VMEM(old.shape, jnp.float32),
            pltpu.VMEM(bus_price.shape, jnp.float32),
            pltpu.SemaphoreType.DMA((3,)),
        ],
        compiler_params=pltpu.CompilerParams(vmem_limit_bytes=24 * 2**20),
        name="lines",
    )(
        pattern,
        *nets,
        blocks,
        limits,
        old,
        pltpu.with_memory_space_constraint(bus_price, pltpu.HBM),
    )


def price_kernel(*refs):
    share_refs, (out_ref, share_all) = refs[:-2], refs[-2:]
    hours = out_ref.shape[0]
    parts = len(share_refs)
    scn_dev = out_ref.shape[1] // parts
    me = lax.axis_index("gen")
    for step, share in enumerate(share_refs):
        share_all[step] = share[...]
    steps = [lax.bitwise_xor(me, part) for part in range(parts)]
    for hour in range(hours):
        less = [share_all[step, hour * scn_dev : (hour + 1) * scn_dev, :] for step in steps]
        out_ref[hour] = -jnp.concatenate(less, axis=0)


def shards(
    bus_price,
    bus_demand,
    multipliers,
    line_limits,
    ptdf_blocks,
    ptdf_pattern,
    gen_bus,
    state_counts,
    transitions,
    state_level,
    state_cost,
):
    scn_dev, hours, bus_dev = bus_demand.shape
    parts = lax.axis_size("gen")
    ring = lax.axis_size("bus")
    half = ring // 2
    gens = state_level.shape[0]
    row_total = scn_dev * hours
    vmem = pl.BlockSpec(memory_space=pltpu.VMEM)
    roomy = pltpu.CompilerParams(vmem_limit_bytes=24 * 2**20)

    def trade(size, step):
        return [(i, i ^ step) for i in range(size)]

    bus_price = jnp.transpose(bus_price, (1, 0, 2))
    bus_demand = jnp.transpose(bus_demand, (1, 0, 2))
    multipliers = jnp.transpose(multipliers, (0, 2, 1, 3))
    transitions = jnp.transpose(transitions, (1, 0, 2))
    ahead = (bus_demand, ptdf_blocks, multipliers, line_limits, ptdf_pattern)
    plan, *ahead = run_plan(
        state_counts, gen_bus, transitions, state_level, state_cost, bus_price, ahead, parts
    )
    bus_demand, ptdf_blocks, multipliers, line_limits, ptdf_pattern = ahead
    received = [plan, lax.ppermute(plan[1:2], "gen", trade(parts, 1))]
    for step in range(2, parts, 2):
        both = lax.ppermute(plan[step : step + 2], "gen", trade(parts, step))
        received += [both, lax.ppermute(both[1:], "gen", trade(parts, 1))]
    net = pl.pallas_call(
        functools.partial(net_kernel, gens=gens),
        out_shape=jax.ShapeDtypeStruct((row_total, bus_dev), jnp.bfloat16),
        in_specs=[vmem] * (len(received) + 1),
        out_specs=vmem,
        compiler_params=roomy,
        name="net",
    )(*received, bus_demand)

    far = [lax.ppermute(net, "bus", trade(ring, 2 * step)) for step in range(1, half)]
    handed = [net] + far
    other = [
        lax.ppermute(net, "bus", trade(ring, 2 * step + 1))
        if step == DIRECT
        else lax.ppermute(handed[step], "bus", trade(ring, 1))
        for step in range(half)
    ]
    new_multipliers, spread, far_part = run_lines(
        ptdf_pattern, [net] + far + other, ptdf_blocks, line_limits, multipliers, bus_price
    )

    own_change = spread[0]
    for step in range(half):
        if step == DIRECT:
            shares = [
                lax.ppermute(far_part[half], "bus", trade(ring, 2 * step)),
                lax.ppermute(far_part[step], "bus", trade(ring, 2 * step + 1)),
            ]
        else:
            shares = [lax.ppermute(far_part[step], "bus", trade(ring, 1))]
            if step:
                share = (spread[step] + shares[0].astype(jnp.float32)).astype(jnp.bfloat16)
                shares = [lax.ppermute(share, "bus", trade(ring, 2 * step))]
        for share in shares:
            own_change = own_change + share.astype(jnp.float32)
    shares = [own_change]
    for step in range(1, parts):
        moved, by = (shares[step - 1], 1) if step % 2 else (own_change, step)
        shares.append(lax.ppermute(moved, "gen", trade(parts, by)))
    new_price = pl.pallas_call(
        price_kernel,
        out_shape=jax.ShapeDtypeStruct(bus_price.shape, jnp.float32),
        in_specs=[vmem] * parts,
        out_specs=vmem,
        scratch_shapes=[pltpu.VMEM((parts, row_total, bus_dev), jnp.float32)],
        compiler_params=roomy,
        name="price",
    )(*shares)
    return (jnp.transpose(new_multipliers, (0, 2, 1, 3)), jnp.transpose(new_price, (1, 0, 2)))


def solution(mesh):
    in_specs = (
        P(None, None, "bus"),
        P("gen", None, "bus"),
        P(None, "gen", None, "bus"),
        P("bus"),
        P("bus", None, None, None),
        P("bus", None),
        P(("gen", "bus")),
        P(("gen", "bus")),
        P(("gen", "bus"), None, None),
        P(("gen", "bus"), None),
        P(("gen", "bus"), None),
    )
    out_specs = (P(None, "gen", None, "bus"), P(None, None, "bus"))
    return jax.shard_map(shards, mesh=mesh, in_specs=in_specs, out_specs=out_specs, check_vma=False)
```

```python
import functools

import jax
import jax.numpy as jnp
from jax import lax
from jax.experimental import pallas as pl
from jax.experimental.pallas import tpu as pltpu
from jax.sharding import PartitionSpec as P

STATES = 512
HALF = 256
BLK = 128
NNZB = 16
GROUP = 16
BIG_GROUP = 6
LANES = 128
AHEAD = 5
DIRECT = 1
SUBLANES = 8


def exact_pieces(values):
    high = values.astype(jnp.bfloat16)
    rest = values - high.astype(jnp.float32)
    middle = rest.astype(jnp.bfloat16)
    low = (rest - middle.astype(jnp.float32)).astype(jnp.bfloat16)
    return jnp.concatenate([high, middle, low], axis=0)


def add_pieces(product):
    count = product.shape[0] // 3
    return product[:count] + (product[count : 2 * count] + product[2 * count :])


def plan_kernel(*refs, gens, parts):
    (counts_hbm, bus_hbm, trans_hbm, level_hbm, cost_hbm, price_hbm), refs = refs[:6], refs[6:]
    ahead_hbm, refs = refs[:AHEAD], refs[AHEAD:]
    out_ref, refs = refs[0], refs[1:]
    ahead_refs, refs = refs[:AHEAD], refs[AHEAD:]
    (
        counts_smem,
        bus_smem,
        trans_ref,
        level_ref,
        cost_ref,
        price_ref,
        order,
        level_slot,
        cost_slot,
        gen_price,
        big_table,
        small_table,
        big_state,
        small_state,
        sems,
    ) = refs
    sources = (counts_hbm, bus_hbm, trans_hbm, level_hbm, cost_hbm, price_hbm) + ahead_hbm
    targets = (counts_smem, bus_smem, trans_ref, level_ref, cost_ref, price_ref) + ahead_refs
    copies = [
        pltpu.make_async_copy(source, target, sems.at[at])
        for at, (source, target) in enumerate(zip(sources, targets))
    ]
    for copy in copies:
        copy.start()
    hours, scn, bus_dev = price_ref.shape
    big_total = BIG_GROUP * (gens // GROUP)
    scn_dev = scn // parts
    per_row = LANES // gens
    for copy in copies[:2]:
        copy.wait()

    def place(gen, taken):
        big = (counts_smem[gen] > HALF).astype(jnp.int32)
        slot = jnp.where(big == 1, taken, gens - 1 - (gen - taken))
        order[slot] = gen
        return taken + big

    lax.fori_loop(0, gens, place, jnp.int32(0))

    for copy in copies[2:6]:
        copy.wait()
    lane = lax.broadcasted_iota(jnp.int32, (1, LANES), 1)
    local_row = jnp.zeros((1, LANES), jnp.int32)
    bus_row = jnp.zeros((1, LANES), jnp.int32)
    for slot in range(gens):
        local = lax.rem(bus_smem[order[slot]], bus_dev)
        local_row = jnp.where(lane == slot, local, local_row)
        bus_row = jnp.where(lane == slot, local, bus_row)
    chooser = (
        lax.broadcasted_iota(jnp.int32, (bus_dev, LANES), 0) == local_row
    ).astype(jnp.bfloat16)
    picked = jnp.dot(
        exact_pieces(price_ref[...].reshape(hours * scn, bus_dev)),
        chooser,
        preferred_element_type=jnp.float32,
    )
    gen_price[...] = add_pieces(picked).reshape(hours, scn, LANES)

    state_ids = lax.broadcasted_iota(jnp.int32, (1, STATES), 1)
    spans = []
    for slot in range(gens):
        gen = order[slot]
        span = STATES if slot < big_total else HALF
        spans.append(span)
        level_slot[slot] = jnp.broadcast_to(level_ref[pl.ds(gen, 1), :], (SUBLANES, STATES))
        cost_row = jnp.where(state_ids < counts_smem[gen], cost_ref[pl.ds(gen, 1), :], 1e30)
        cost_slot[slot] = jnp.broadcast_to(cost_row, (SUBLANES, STATES))
        successors = [trans_ref[branch, pl.ds(gen, 1), :] for branch in range(trans_ref.shape[0])]
        table = big_table.at[slot] if slot < big_total else small_table.at[slot - big_total]
        for first in range(0, span, HALF):
            rows = lax.broadcasted_iota(jnp.int32, (HALF, span), 0).astype(jnp.float32).astype(jnp.bfloat16)
            one = jnp.ones((HALF, span), jnp.bfloat16)
            none = jnp.zeros((HALF, span), jnp.bfloat16)
            total = none
            for row in successors:
                shifted = (row[:, :span] - first).astype(jnp.float32).astype(jnp.bfloat16)
                total = total + jnp.where(rows == shifted, one, none)
            table[pl.ds(first, HALF), :] = total

    def repeat_rows(block, copies):
        return block if copies == 1 else jnp.concatenate([block] * copies, axis=0)

    mixed = sorted(
        range(gens),
        key=lambda slot: (slot + 0.5) / big_total
        if slot < big_total
        else (slot - big_total + 0.5) / (gens - big_total),
    )
    shares = [None] * gens
    outs = [jnp.zeros((scn, LANES), jnp.float32) for _ in range(-(-hours // per_row))]
    for hour in range(hours - 1, -1, -1):
        chains = hours - 1 - hour
        for slot in mixed:
            span = spans[slot]
            if slot < big_total:
                state, table = big_state.at[slot], big_table.at[slot]
            else:
                state, table = small_state.at[slot - big_total], small_table.at[slot - big_total]
            level = repeat_rows(level_slot[slot][:, :span], scn // SUBLANES)
            cost = repeat_rows(cost_slot[slot][:, :span], scn // SUBLANES)
            price = gen_price[hour][:, slot : slot + 1]
            weight = jnp.exp(price * level - cost)
            if chains > 0:
                weight = weight * shares[slot]
            base = weight if chains == 0 else weight * state[:scn, :]
            total = jnp.sum(base, axis=-1, keepdims=True)
            if hour > 0:
                shares[slot] = 1.0 / total
                pieces = [base.astype(jnp.bfloat16)]
                for chain in range(chains):
                    pieces.append(
                        (weight * state[(chain + 1) * scn : (chain + 2) * scn, :]).astype(jnp.bfloat16)
                    )
                pieces.append((base * level).astype(jnp.bfloat16))
                moved = jnp.dot(
                    jnp.concatenate(pieces, axis=0), table[...], preferred_element_type=jnp.float32
                )
                state[: (chains + 2) * scn, :] = moved
            else:
                for at in range(hours):
                    if at == 0:
                        marked = base * level
                    else:
                        chain = hours - 1 - at
                        marked = weight * state[(chain + 1) * scn : (chain + 2) * scn, :]
                    mean = jnp.sum(marked, axis=-1, keepdims=True) / total
                    here = lane == (at % per_row) * gens + slot
                    outs[at // per_row] = jnp.where(here, mean, outs[at // per_row])
    me = lax.axis_index("gen")
    for slot in range(gens):
        here = lane == (hours % per_row) * gens + slot
        bus = jnp.sum(jnp.where(lane == slot, bus_row, 0)).astype(jnp.float32)
        outs[-1] = jnp.where(here, bus, outs[-1])
    for part in range(parts):
        for row, block in enumerate(outs):
            out_ref[lax.bitwise_xor(me, part), row] = block[part * scn_dev : (part + 1) * scn_dev, :]
    for copy in copies[6:]:
        copy.wait()


def run_plan(counts, gen_bus, transitions, level, cost, bus_price, ahead, parts):
    hours, scn, _ = bus_price.shape
    gens = level.shape[0]
    big_total = BIG_GROUP * (gens // GROUP)
    rows = -(-hours // (LANES // gens))
    hbm = pl.BlockSpec(memory_space=pltpu.HBM)
    vmem = pl.BlockSpec(memory_space=pltpu.VMEM)
    return pl.pallas_call(
        functools.partial(plan_kernel, gens=gens, parts=parts),
        out_shape=(pltpu.VMEM((parts, rows, scn // parts, LANES), jnp.float32),)
        + tuple(pltpu.VMEM(array.shape, array.dtype) for array in ahead),
        in_specs=[hbm] * (6 + len(ahead)),
        out_specs=(vmem,) * (1 + len(ahead)),
        scratch_shapes=[
            pltpu.SMEM(counts.shape, jnp.int32),
            pltpu.SMEM(gen_bus.shape, jnp.int32),
            pltpu.VMEM(transitions.shape, jnp.int32),
            pltpu.VMEM(level.shape, jnp.float32),
            pltpu.VMEM(cost.shape, jnp.float32),
            pltpu.VMEM(bus_price.shape, jnp.float32),
            pltpu.SMEM((gens,), jnp.int32),
            pltpu.VMEM((gens, SUBLANES, STATES), jnp.float32),
            pltpu.VMEM((gens, SUBLANES, STATES), jnp.float32),
            pltpu.VMEM((hours, scn, LANES), jnp.float32),
            pltpu.VMEM((big_total, STATES, STATES), jnp.bfloat16),
            pltpu.VMEM((gens - big_total, HALF, HALF), jnp.bfloat16),
            pltpu.VMEM((big_total, (hours + 1) * scn, STATES), jnp.float32),
            pltpu.VMEM((gens - big_total, (hours + 1) * scn, HALF), jnp.float32),
            pltpu.SemaphoreType.DMA((6 + len(ahead),)),
        ],
        compiler_params=pltpu.CompilerParams(vmem_limit_bytes=32 * 2**20),
        name="plan",
    )(
        *(
            pltpu.with_memory_space_constraint(array, pltpu.HBM)
            for array in (counts, gen_bus, transitions, level, cost, bus_price) + ahead
        )
    )


def net_kernel(*refs, gens):
    plan_refs, (demand_ref, net_ref) = refs[:-2], refs[-2:]
    rows, scn_dev = plan_refs[0].shape[1:3]
    hours, _, bus_dev = demand_ref.shape
    per_row = LANES // gens
    lane = lax.broadcasted_iota(jnp.int32, (1, LANES), 1)
    bus_ids = lax.broadcasted_iota(jnp.int32, (bus_dev, LANES), 0).astype(jnp.float32)

    def of_hour(hour):
        start = (hour % per_row) * gens
        return (lane >= start) & (lane < start + gens)

    left, places = [], []
    for plan_ref in plan_refs:
        values = [plan_ref[0, row] for row in range(rows)]
        left.append(
            jnp.concatenate(
                [jnp.where(of_hour(hour), values[hour // per_row], 0.0) for hour in range(hours)], axis=0
            )
        )
        bus = jnp.where(of_hour(hours), values[-1][:1, :], 0.0)
        bus = jnp.broadcast_to(bus, (SUBLANES, LANES))
        shift = gens
        while shift < LANES:
            bus = bus + pltpu.roll(bus, shift, 1)
            shift *= 2
        places.append((bus_ids == bus[:1, :]).astype(jnp.bfloat16))
    left = jnp.concatenate(left, axis=1)
    placed = lax.dot_general(
        exact_pieces(left),
        jnp.concatenate(places, axis=1),
        (((1,), (1,)), ((), ())),
        preferred_element_type=jnp.float32,
    )
    injections = add_pieces(placed)
    demand = jnp.concatenate([demand_ref[hour] for hour in range(hours)], axis=0)
    net_ref[...] = (injections - demand).astype(jnp.bfloat16)


def line_kernel(pattern_ref, *refs, half):
    net_refs, refs = refs[: 2 * half], refs[2 * half :]
    blocks_ref, limits_ref, old_ref, price_hbm, new_hbm, spread_all, far_out = refs[:7]
    pattern_smem, net_all, new_ref, price_ref, sems = refs[7:]
    pattern_copy = pltpu.make_async_copy(pattern_ref, pattern_smem, sems.at[2])
    pattern_copy.start()
    price_copy = pltpu.make_async_copy(price_hbm, price_ref, sems.at[0])
    price_copy.start()
    new_copy = pltpu.make_async_copy(new_ref, new_hbm, sems.at[1])
    line_blocks, branches = pattern_ref.shape
    _, hours, scn_dev, _ = old_ref.shape
    bus_dev = net_refs[0].shape[1]
    per_dev = bus_dev // BLK
    me = lax.axis_index("bus")
    my_pair, my_side = me // 2, lax.rem(me, 2)

    for at, net_ref in enumerate(net_refs):
        net_all[at] = net_ref[...]
    spread_all[...] = jnp.zeros(spread_all.shape, jnp.float32)
    pattern_copy.wait()

    def spot(line, branch):
        block = pattern_smem[line, branch]
        owner = block // per_dev
        column = pl.multiple_of(lax.rem(block, per_dev) * BLK, BLK)
        step = lax.bitwise_xor(my_pair, owner // 2)
        side = jnp.where(lax.rem(owner, 2) == my_side, 0, half)
        return side + step, column

    spots = [[spot(line, branch) for branch in range(branches)] for line in range(line_blocks)]
    tables = [blocks_ref.at[line] for line in range(line_blocks)]
    changes = []
    for line in range(line_blocks):
        picked = [net_all[at, :, pl.ds(column, BLK)] for at, column in spots[line]]
        flow = jnp.dot(
            jnp.concatenate(picked, axis=1),
            tables[line][...].reshape(branches * BLK, BLK),
            preferred_element_type=jnp.float32,
        )
        lanes = pl.ds(line * BLK, BLK)
        limit = limits_ref[lanes].reshape(1, BLK)
        upper_old = jnp.concatenate([old_ref[0, hour, :, lanes] for hour in range(hours)], axis=0)
        lower_old = jnp.concatenate([old_ref[1, hour, :, lanes] for hour in range(hours)], axis=0)
        upper = jnp.maximum(0.0, upper_old + (flow - limit))
        lower = jnp.maximum(0.0, lower_old + (-flow - limit))
        for hour in range(hours):
            here = slice(hour * scn_dev, (hour + 1) * scn_dev)
            new_ref[0, hour, :, lanes] = upper[here]
            new_ref[1, hour, :, lanes] = lower[here]
        changes.append(((upper - upper_old) - (lower - lower_old)).astype(jnp.bfloat16))
    new_copy.start()
    for line in range(line_blocks):
        spread = lax.dot_general(
            changes[line],
            tables[line][...].reshape(branches * BLK, BLK),
            (((1,), (1,)), ((), ())),
            preferred_element_type=jnp.float32,
        )
        held = [spread_all[at, :, pl.ds(column, BLK)] for at, column in spots[line]]
        for branch, (at, column) in enumerate(spots[line]):
            spread_all[at, :, pl.ds(column, BLK)] = (
                held[branch] + spread[:, branch * BLK : (branch + 1) * BLK]
            )
    far_out[:half] = spread_all[half:].astype(jnp.bfloat16)
    far_out[half] = spread_all[DIRECT].astype(jnp.bfloat16)
    price_copy.wait()
    part = lax.axis_index("gen")
    for hour in range(hours):
        price = price_ref[hour, :scn_dev, :]
        for other in range(1, price_ref.shape[1] // scn_dev):
            price = jnp.where(part == other, price_ref[hour, other * scn_dev : (other + 1) * scn_dev, :], price)
        here = slice(hour * scn_dev, (hour + 1) * scn_dev)
        spread_all[0, here, :] = spread_all[0, here, :] - price
    new_copy.wait()


def run_lines(pattern, nets, blocks, limits, old, bus_price):
    ring = len(nets)
    half = ring // 2
    vmem = pl.BlockSpec(memory_space=pltpu.VMEM)
    hbm = pl.BlockSpec(memory_space=pltpu.HBM)
    return pl.pallas_call(
        functools.partial(line_kernel, half=half),
        out_shape=(
            jax.ShapeDtypeStruct(old.shape, jnp.float32),
            jax.ShapeDtypeStruct((ring,) + nets[0].shape, jnp.float32),
            jax.ShapeDtypeStruct((half + 1,) + nets[0].shape, jnp.bfloat16),
        ),
        in_specs=[vmem] * (ring + 4) + [hbm],
        out_specs=(hbm, vmem, vmem),
        scratch_shapes=[
            pltpu.SMEM(pattern.shape, jnp.int32),
            pltpu.VMEM((ring,) + nets[0].shape, jnp.bfloat16),
            pltpu.VMEM(old.shape, jnp.float32),
            pltpu.VMEM(bus_price.shape, jnp.float32),
            pltpu.SemaphoreType.DMA((3,)),
        ],
        compiler_params=pltpu.CompilerParams(vmem_limit_bytes=24 * 2**20),
        name="lines",
    )(
        pattern,
        *nets,
        blocks,
        limits,
        old,
        pltpu.with_memory_space_constraint(bus_price, pltpu.HBM),
    )


def price_kernel(*refs):
    share_refs, (out_ref, share_all) = refs[:-2], refs[-2:]
    hours = out_ref.shape[0]
    parts = len(share_refs)
    scn_dev = out_ref.shape[1] // parts
    me = lax.axis_index("gen")
    for step, share in enumerate(share_refs):
        share_all[step] = share[...]
    steps = [lax.bitwise_xor(me, part) for part in range(parts)]
    for hour in range(hours):
        less = [share_all[step, hour * scn_dev : (hour + 1) * scn_dev, :] for step in steps]
        out_ref[hour] = -jnp.concatenate(less, axis=0)


def shards(
    bus_price,
    bus_demand,
    multipliers,
    line_limits,
    ptdf_blocks,
    ptdf_pattern,
    gen_bus,
    state_counts,
    transitions,
    state_level,
    state_cost,
):
    scn_dev, hours, bus_dev = bus_demand.shape
    parts = lax.axis_size("gen")
    ring = lax.axis_size("bus")
    half = ring // 2
    gens = state_level.shape[0]
    row_total = scn_dev * hours
    vmem = pl.BlockSpec(memory_space=pltpu.VMEM)
    roomy = pltpu.CompilerParams(vmem_limit_bytes=24 * 2**20)

    def trade(size, step):
        return [(i, i ^ step) for i in range(size)]

    bus_price = jnp.transpose(bus_price, (1, 0, 2))
    bus_demand = jnp.transpose(bus_demand, (1, 0, 2))
    multipliers = jnp.transpose(multipliers, (0, 2, 1, 3))
    transitions = jnp.transpose(transitions, (1, 0, 2))
    ahead = (bus_demand, ptdf_blocks, multipliers, line_limits, ptdf_pattern)
    plan, *ahead = run_plan(
        state_counts, gen_bus, transitions, state_level, state_cost, bus_price, ahead, parts
    )
    bus_demand, ptdf_blocks, multipliers, line_limits, ptdf_pattern = ahead
    received = [plan, lax.ppermute(plan[1:2], "gen", trade(parts, 1))]
    for step in range(2, parts, 2):
        both = lax.ppermute(plan[step : step + 2], "gen", trade(parts, step))
        received += [both, lax.ppermute(both[1:], "gen", trade(parts, 1))]
    net = pl.pallas_call(
        functools.partial(net_kernel, gens=gens),
        out_shape=jax.ShapeDtypeStruct((row_total, bus_dev), jnp.bfloat16),
        in_specs=[vmem] * (len(received) + 1),
        out_specs=vmem,
        compiler_params=roomy,
        name="net",
    )(*received, bus_demand)

    far = [lax.ppermute(net, "bus", trade(ring, 2 * step)) for step in range(1, half)]
    handed = [net] + far
    other = [
        lax.ppermute(net, "bus", trade(ring, 2 * step + 1))
        if step == DIRECT
        else lax.ppermute(handed[step], "bus", trade(ring, 1))
        for step in range(half)
    ]
    new_multipliers, spread, far_part = run_lines(
        ptdf_pattern, [net] + far + other, ptdf_blocks, line_limits, multipliers, bus_price
    )

    own_change = spread[0]
    for step in range(half):
        if step == DIRECT:
            shares = [
                lax.ppermute(far_part[half], "bus", trade(ring, 2 * step)),
                lax.ppermute(far_part[step], "bus", trade(ring, 2 * step + 1)),
            ]
        else:
            shares = [lax.ppermute(far_part[step], "bus", trade(ring, 1))]
            if step:
                share = (spread[step] + shares[0].astype(jnp.float32)).astype(jnp.bfloat16)
                shares = [lax.ppermute(share, "bus", trade(ring, 2 * step))]
        for share in shares:
            own_change = own_change + share.astype(jnp.float32)
    shares = [own_change]
    for step in range(1, parts):
        moved, by = (shares[step - 1], 1) if step % 2 else (own_change, step)
        shares.append(lax.ppermute(moved, "gen", trade(parts, by)))
    new_price = pl.pallas_call(
        price_kernel,
        out_shape=jax.ShapeDtypeStruct(bus_price.shape, jnp.float32),
        in_specs=[vmem] * parts,
        out_specs=vmem,
        scratch_shapes=[pltpu.VMEM((parts, row_total, bus_dev), jnp.float32)],
        compiler_params=roomy,
        name="price",
    )(*shares)
    return (jnp.transpose(new_multipliers, (0, 2, 1, 3)), jnp.transpose(new_price, (1, 0, 2)))


def solution(mesh):
    in_specs = (
        P(None, None, "bus"),
        P("gen", None, "bus"),
        P(None, "gen", None, "bus"),
        P("bus"),
        P("bus", None, None, None),
        P("bus", None),
        P(("gen", "bus")),
        P(("gen", "bus")),
        P(("gen", "bus"), None, None),
        P(("gen", "bus"), None),
        P(("gen", "bus"), None),
    )
    out_specs = (P(None, "gen", None, "bus"), P(None, None, "bus"))
    return jax.shard_map(shards, mesh=mesh, in_specs=in_specs, out_specs=out_specs, check_vma=False)
```
